256 devices in a mesh: ta: 4 (over x_lo, core), ha: 8 (over z), wa: 8 (over x_hi, y).
Axes of the slice: x: 4 (x_hi: 2, x_lo: 2; x = x_hi * 2 + x_lo), y: 4, z: 8, core: 2. Of those that a mesh axis runs over, the one named last changes fastest.
Arguments:
- queries: bfloat16 [4, 8, 16, 1, 384, 128], P('ta', 'ha', 'wa'), may hold values from -6 to 6
- key_tiles: bfloat16 [4, 8, 16, 1, 384, 128], P('ta', 'ha', 'wa'), may hold values from -6 to 6
- value_tiles: bfloat16 [4, 8, 16, 1, 384, 128], P('ta', 'ha', 'wa'), may hold values from -6 to 6
- forward_out: bfloat16 [4, 8, 16, 1, 384, 128], P('ta', 'ha', 'wa'), may hold values from -6 to 6
- out_grad: bfloat16 [4, 8, 16, 1, 384, 128], P('ta', 'ha', 'wa'), may hold values from -96 to 96
- pattern: int32 [1, 27], replicated, may hold values 0 or 1
- tile_active: int32 [4, 8, 16], replicated, may hold values 0 or 1
Outputs:
- query_grad: bfloat16 [4, 8, 16, 1, 384, 128], P('ta', 'ha', 'wa')
- key_grad: bfloat16 [4, 8, 16, 1, 384, 128], P('ta', 'ha', 'wa')
- value_grad: bfloat16 [4, 8, 16, 1, 384, 128], P('ta', 'ha', 'wa')
The draws below stay inside these ranges and needn't reach their ends.
All inputs are finite; a program needn't handle non-finite values.
Results may differ from the reference program's by a relative error of at most 0.0065.
Values may be sent and summed in bfloat16 or wider, within the bound.
A program may use at most 64 MiB of HBM per device.

```python
import math
import jax
import jax.numpy as jnp
import numpy as np
from jax import lax

TILE = 384
HEAD_DIM = 128
HEADS = 1
NT = 4
NH = 8
NW = 16


def draw_queries(key, part):
    key = jax.random.fold_in(key, 1)
    full_shape = (NT, NH, NW, HEADS, TILE, HEAD_DIM)
    values_drawn = jnp.clip(jax.random.normal(key, full_shape, jnp.float32) * 1.2, -6.0, 6.0)
    return values_drawn.astype(jnp.bfloat16)


def draw_key_tiles(key, part):
    key = jax.random.fold_in(key, 2)
    full_shape = (NT, NH, NW, HEADS, TILE, HEAD_DIM)
    values_drawn = jnp.clip(jax.random.normal(key, full_shape, jnp.float32) * 1.25, -6.0, 6.0)
    return values_drawn.astype(jnp.bfloat16)


def with_ends(values, stream_key, low, high):
    dims = values.shape
    spot = [jax.random.randint(jax.random.fold_in(stream_key, axis), (), 0, dims[axis]) for axis in range(len(dims))]
    values = values.at[tuple(spot)].set(low)
    longest = dims.index(max(dims))
    spot[longest] = (spot[longest] + 1) % dims[longest]
    return values.at[tuple(spot)].set(high)


def block_scale(key, extent, split, least, top_value):
    def one(axis_at, shards_of):
        draws = jax.random.uniform(jax.random.fold_in(jax.random.fold_in(key, 6), axis_at), (shards_of,), jnp.float32, least / len(split), top_value / len(split))
        return jnp.repeat(jnp.exp(draws), extent[axis_at] // shards_of).reshape((-1,) + (1,) * (len(extent) - axis_at - 1))

    loudness = one(*split[0])
    for cut in split[1:]:
        loudness = loudness * one(*cut)
    return loudness


def gaussian(key, shape, scale, reach, pieces=(), kind=jnp.bfloat16):
    drawn = scale * jax.random.normal(key, shape, jnp.float32)
    if pieces:
        drawn = drawn * block_scale(key, shape, pieces, -0.22, 0.18)
    return jnp.clip(drawn, -reach, reach).astype(kind)


def setup_inputs(seed: int = 0) -> dict:
    key_of = jax.random.split(jax.random.key(seed), 8)
    return {
        "queries": draw_queries(jax.random.fold_in(key_of[7], 71), 0),
        "key_tiles": draw_key_tiles(jax.random.fold_in(key_of[7], 71), 0),
        "value_tiles": gaussian(key_of[2], (NT, NH, NW, HEADS, TILE, HEAD_DIM), 1.0, 6.0, ((0, 4), (1, 8), (2, 8))),
        "forward_out": gaussian(key_of[3], (NT, NH, NW, HEADS, TILE, HEAD_DIM), 1.0, 6.0, ((0, 4), (1, 8), (2, 8))),
        "out_grad": gaussian(key_of[4], (NT, NH, NW, HEADS, TILE, HEAD_DIM), 16.0, 96.0, ((0, 4), (1, 8), (2, 8))),
        "pattern": with_ends((jax.random.randint(key_of[5], (HEADS, 27), 0, 2) < 1).astype(jnp.int32), jax.random.fold_in(key_of[5], 1), 0, 1),
        "tile_active": with_ends((jax.random.randint(key_of[6], (NT, NH, NW), 0, 4) < 3).astype(jnp.int32), jax.random.fold_in(key_of[6], 1), 0, 1),
    }


side_offsets = np.array([place for place in range(27) if place != 13], np.int32)

def as_index(value):
    return jnp.asarray(value, dtype=jnp.int32)

def block_at(extended, offset, tile_span):
    offset = as_index(offset)
    first_time = offset // 9
    first_height = offset // 3 % 3
    first_width = offset % 3
    starts = (first_time, first_height, first_width) + tuple((as_index(0) for _ in range(extended.ndim - 3)))
    block_shape = tuple(tile_span) + tuple(extended.shape[3:])
    return lax.dynamic_slice(extended, starts, block_shape)

def allowed_mask(inside_ext, active_ext, pattern, offset, tile_span):
    offset = as_index(offset)
    inside_here = block_at(inside_ext, offset, tile_span)
    active_here = block_at(active_ext, offset, tile_span)
    chosen = lax.dynamic_index_in_dim(pattern, offset, axis=1, keepdims=False)
    listed = (chosen[None, None, None, :] == 1) & (active_here[..., None] == 1)
    return (inside_here[..., None] == 1) & ((offset == 13) | listed)

def product(form, left, right):
    return jnp.einsum(form, left.astype(jnp.float32), right.astype(jnp.float32))

def tile_scores(queries, key_block, score_scale):
    return product('abceid,abcejd->abceij', queries, key_block) * score_scale

def softmax_stats(queries, key_ext, inside_ext, active_ext, pattern, tile_span, score_scale):
    centre = tile_scores(queries, block_at(key_ext, 13, tile_span), score_scale)
    running_top = lax.optimization_barrier(jnp.max(centre, axis=-1))
    running_sum = lax.optimization_barrier(jnp.sum(jnp.exp(centre - running_top[..., None]), axis=-1))

    def advance(carried, offset):
        old_top, old_sum = carried
        allowed = allowed_mask(inside_ext, active_ext, pattern, offset, tile_span)[..., None, None]
        scores = tile_scores(queries, block_at(key_ext, offset, tile_span), score_scale)
        masked = jnp.where(allowed, scores, -jnp.inf)
        raised_top = jnp.maximum(old_top, lax.optimization_barrier(jnp.max(masked, axis=-1)))
        new_sum = old_sum * jnp.exp(old_top - raised_top) + lax.optimization_barrier(jnp.sum(jnp.exp(masked - raised_top[..., None]), axis=-1))
        return ((raised_top, new_sum), None)
    (running_top, running_sum), _ = lax.scan(advance, (running_top, running_sum), jnp.asarray(side_offsets, dtype=jnp.int32))
    return running_top + jnp.log(running_sum)

def backward_pass(queries, out_grad, key_ext, value_ext, log_total, out_dot, inside_ext, active_ext, pattern, tile_span, score_scale):
    query_acc = jnp.zeros(queries.shape, queries.dtype if False else jnp.float32)
    pair_acc = jnp.zeros((2,) + key_ext.shape, jnp.float32)

    def advance(carried, offset):
        query_sum, pair_sum = carried
        offset = as_index(offset)
        allowed = allowed_mask(inside_ext, active_ext, pattern, offset, tile_span)[..., None, None]
        key_block = block_at(key_ext, offset, tile_span)
        value_block = block_at(value_ext, offset, tile_span)
        scores = tile_scores(queries, key_block, score_scale)
        probs_full = jnp.where(allowed, jnp.exp(scores - log_total[..., None]), 0.0)
        prob_grad = product('abceid,abcejd->abceij', out_grad, value_block)
        score_grad = probs_full * (prob_grad - out_dot[..., None])
        probs_low = probs_full.astype(jnp.bfloat16)
        score_low = score_grad.astype(jnp.bfloat16)
        query_sum = query_sum + product('abceij,abcejd->abceid', score_low, key_block) * score_scale
        key_part = product('abceij,abceid->abcejd', score_low, queries) * score_scale
        value_part = product('abceij,abceid->abcejd', probs_low, out_grad)
        update = jnp.stack([key_part, value_part]).astype(pair_sum.dtype)
        zero = as_index(0)
        starts = (zero, offset // 9, offset // 3 % 3, offset % 3, zero, zero, zero)
        current = lax.dynamic_slice(pair_sum, starts, update.shape)
        pair_sum = lax.dynamic_update_slice(pair_sum, current + update, starts)
        return ((query_sum, pair_sum), None)
    (query_acc, pair_acc), _ = lax.scan(advance, (query_acc, pair_acc), jnp.arange(27, dtype=jnp.int32))
    return (query_acc, pair_acc)

def reference(queries, key_tiles, value_tiles, forward_out, out_grad, pattern, tile_active):
    score_scale = 1.0 / math.sqrt(queries.shape[5])
    tile_span = queries.shape[:3]
    pad_widths = ((1, 1), (1, 1), (1, 1), (0, 0), (0, 0), (0, 0))
    key_ext = jnp.pad(key_tiles, pad_widths)
    value_ext = jnp.pad(value_tiles, pad_widths)
    active_ext = jnp.pad(tile_active, 1)
    inside_ext = jnp.pad(jnp.ones_like(tile_active), 1)
    out_dot = lax.optimization_barrier(jnp.sum(out_grad.astype(jnp.float32) * forward_out.astype(jnp.float32), axis=-1))
    log_total = softmax_stats(queries, key_ext, inside_ext, active_ext, pattern, tile_span, score_scale)
    query_acc, pair_acc = backward_pass(queries, out_grad, key_ext, value_ext, log_total, out_dot, inside_ext, active_ext, pattern, tile_span, score_scale)
    interior = pair_acc[:, 1:-1, 1:-1, 1:-1]
    return (query_acc.astype(jnp.bfloat16), interior[0].astype(jnp.bfloat16), interior[1].astype(jnp.bfloat16))
```

```python
import functools
import math

import jax
import jax.numpy as jnp
from jax import lax
from jax.experimental import pallas as pl
from jax.experimental.pallas import tpu as pltpu
from jax.sharding import PartitionSpec as P

MESH = pl.DeviceIdType.MESH
F32 = jnp.float32
BF16 = jnp.bfloat16
NT = (((1,), (1,)), ((), ()))
TN = (((0,), (0,)), ((), ()))
NN = (((1,), (0,)), ((), ()))
LOW = -1e30
TOGETHER = 3


def dot(left, right, form):
    return lax.dot_general(left, right, form, preferred_element_type=F32)


def position():
    return lax.axis_index("ta"), lax.axis_index("ha"), lax.axis_index("wa")


class Links:
    def __init__(self, sizes, send_sem, recv_sem):
        self.sizes = sizes
        self.at = position()
        self.send_sem = send_sem
        self.recv_sem = recv_sem

    def there(self, step):
        found = None
        for place, size, by in zip(self.at, self.sizes, step):
            if by:
                ok = (place + by >= 0) & (place + by < size)
                found = ok if found is None else found & ok
        return found

    def device(self, step):
        return tuple(
            lax.rem(place + by + size, size) for place, size, by in zip(self.at, self.sizes, step)
        )

    def greet(self, steps):
        barrier = pltpu.get_barrier_semaphore()
        count = 0
        for step in steps:
            count = count + self.there(step).astype(jnp.int32)

            @pl.when(self.there(step))
            def _():
                pl.semaphore_signal(
                    barrier, inc=1, device_id=self.device(step), device_id_type=MESH
                )

        pl.semaphore_wait(barrier, count)

    def copy(self, src, dst, number, step):
        return pltpu.make_async_remote_copy(
            src_ref=src,
            dst_ref=dst,
            send_sem=self.send_sem.at[number],
            recv_sem=self.recv_sem.at[number],
            device_id=self.device(step),
            device_id_type=MESH,
        )


def back(step):
    return tuple(-by for by in step)


W_UP, W_DOWN, T_UP, T_DOWN, H_UP, H_DOWN = (
    (0, 0, 1),
    (0, 0, -1),
    (1, 0, 0),
    (-1, 0, 0),
    (0, 1, 0),
    (0, -1, 0),
)


def gather_kernel(sizes, q, do, k, v, qa, doa, ka, va, local_sem, send_sem, recv_sem):
    links = Links(sizes, send_sem, recv_sem)
    there = links.there
    links.greet([W_UP, W_DOWN, T_UP, T_DOWN, H_UP, H_DOWN])
    locals_ = []
    plain = []
    relays = []
    number = 0
    for turn, (rows, rows_all, cols, cols_all) in enumerate(((q, qa, k, ka), (do, doa, v, va))):
        to_right = links.copy(rows.at[1], rows_all.at[1, 0], number, W_UP)
        to_left = links.copy(rows.at[0], rows_all.at[1, 3], number + 1, W_DOWN)
        plain += [
            (to_right, there(W_UP), None),
            (to_left, there(W_DOWN), None),
            (links.copy(rows, rows_all.at[0, pl.ds(1, 2)], number + 2, T_UP), there(T_UP), there(T_DOWN)),
            (links.copy(rows, rows_all.at[2, pl.ds(1, 2)], number + 3, T_DOWN), there(T_DOWN), there(T_UP)),
            (links.copy(cols, cols_all.at[0], number + 4, H_UP), there(H_UP), there(H_DOWN)),
            (links.copy(cols, cols_all.at[2], number + 5, H_DOWN), there(H_DOWN), there(H_UP)),
        ]
        number += 6
        for came, spot, has in ((to_right, 0, there(W_DOWN)), (to_left, 3, there(W_UP))):
            fans = []
            for step, slot in ((T_UP, 0), (T_DOWN, 2)):
                fan = links.copy(rows_all.at[1, spot], rows_all.at[slot, spot], number, step)
                fans.append((fan, has & there(step), has & there(back(step))))
                number += 1
            relays.append((came, has, fans))
        locals_ += [
            pltpu.make_async_copy(rows, rows_all.at[1, pl.ds(1, 2)], local_sem.at[2 * turn]),
            pltpu.make_async_copy(cols, cols_all.at[1], local_sem.at[2 * turn + 1]),
        ]
    for copy, goes, _ in plain:
        pl.when(goes)(copy.start)
    for copy in locals_:
        copy.start()
    for came, has, fans in relays:
        pl.when(has)(came.wait_recv)
        for fan, goes, _ in fans:
            pl.when(goes)(fan.start)
    for copy, goes, comes in plain + [fan for _, _, fans in relays for fan in fans]:
        pl.when(goes)(copy.wait_send)
        if comes is not None:
            pl.when(comes)(copy.wait_recv)
    for copy in locals_:
        copy.wait()


def list_pairs(sizes, pattern, active, pairs):
    t, h, w = position()
    nt, nh, nw = sizes

    def keys(place, count):
        row, col = place // 2, place % 2
        key_in = (h + row - 1 >= 0) & (h + row - 1 < nh)
        key_h = jnp.clip(h + row - 1, 0, nh - 1)
        lit = active[t * nh + key_h, 2 * w + col]
        for time in range(3):
            time_in = (t + time - 1 >= 0) & (t + time - 1 < nt)
            for shift in range(3):
                spot = col + 2 - shift
                inside = key_in & time_in & (2 * w + spot - 1 >= 0) & (2 * w + spot - 1 < 2 * nw)
                offset = 9 * (2 - time) + 3 * row + shift
                chosen = (pattern[0, offset] == 1) & (lit == 1)
                pairs[count] = place * 12 + time * 4 + spot
                count = count + (inside & (chosen | (offset == 13))).astype(jnp.int32)
        return count

    return lax.fori_loop(0, 6, keys, jnp.int32(0))


def pair_at(pairs, count, index):
    real = index < count
    code = jnp.where(real, pairs[jnp.minimum(index, count - 1)], 0)
    key, query = code // 12, code % 12
    return key, query, jnp.where(real, key, 6), jnp.where(real, query, 12)


def stats_kernel(sizes, factor, pattern, active, q, k, do, fo, out, pairs, acc):
    count = list_pairs(sizes, pattern, active, pairs)
    acc[:, 0:1, :] = jnp.full((13, 1, acc.shape[2]), LOW, F32)
    acc[:, 1:8, :] = jnp.zeros((13, 7, acc.shape[2]), F32)
    for tile in range(2):
        both = do[tile].astype(F32) * fo[tile].astype(F32)
        acc[5 + tile, 2:3, :] = jnp.sum(both.T, axis=0, keepdims=True)

    def some(group, carried):
        spots = [pair_at(pairs, count, group * TOGETHER + x) for x in range(TOGETHER)]
        scores = [dot(k[key], q[query], NT) * factor for key, query, _, _ in spots]
        tops = [jnp.max(x, axis=0, keepdims=True) for x in scores]
        sums = [jnp.sum(jnp.exp2(x - top), axis=0, keepdims=True) for x, top in zip(scores, tops)]
        for (_, _, _, query), top, total in zip(spots, tops, sums):
            old = acc[query, 0:1, :]
            new = jnp.maximum(old, top)
            acc[query, 1:2, :] = acc[query, 1:2, :] * jnp.exp2(old - new) + total * jnp.exp2(top - new)
            acc[query, 0:1, :] = new
        return carried

    lax.fori_loop(0, pl.cdiv(count, TOGETHER), some, 0)
    out[...] = acc[0:12]


PLANE = [(dt, dw) for dt in (-1, 0, 1) for dw in (-1, 0, 1) if (dt, dw) != (0, 0)]


def totals_kernel(sizes, part, out, inbox, send_sem, recv_sem):
    links = Links(sizes, send_sem, recv_sem)
    links.greet([(dt, 0, dw) for dt, dw in PLANE])
    first = []
    second = []
    for number, (dt, dw) in enumerate(PLANE):
        step = (dt, 0, dw)
        goes, comes = links.there(step), links.there(back(step))
        if dw == 0:
            src, dst = part.at[1 + dt, pl.ds(1, 2)], inbox.at[number]
            own, far = out.at[1, pl.ds(1, 2)], out.at[1 - dt, pl.ds(1, 2)]
        elif dw == 1:
            src, dst = part.at[1 + dt, 3], inbox.at[number, 0]
            own, far = out.at[1, 2], out.at[1 - dt, 0]
        else:
            src, dst = part.at[1 + dt, 0], inbox.at[number, 1]
            own, far = out.at[1, 1], out.at[1 - dt, 3]
        copy = links.copy(src, dst, number, step)
        pl.when(goes)(copy.start)
        first.append((copy, goes, comes, dst))
        second.append((links.copy(own, far, 8 + number, step), goes, comes))
    for copy, goes, comes, dst in first:

        @pl.when(jnp.logical_not(comes))
        def _():
            dst[...] = jnp.full(dst.shape, LOW, F32)

        pl.when(comes)(copy.wait_recv)
    for tile in range(2):
        terms = [(part[1, 1 + tile, 0:1, :], part[1, 1 + tile, 1:2, :])]
        for number, (dt, dw) in enumerate(PLANE):
            if dw == 0 or dw == 1 - 2 * tile:
                total = inbox[number, tile, 1:2, :]
                terms.append((inbox[number, tile, 0:1, :], jnp.maximum(total, 0.0)))
        top = functools.reduce(jnp.maximum, [x for x, _ in terms])
        total = sum(x * jnp.exp2(y - top) for y, x in terms)
        out[1, 1 + tile, 0:1, :] = top + jnp.log2(total)
        out[1, 1 + tile, 1:2, :] = part[1, 1 + tile, 2:3, :]
        out[1, 1 + tile, 2:8, :] = jnp.zeros((6, out.shape[3]), F32)
    for copy, goes, _ in second:
        pl.when(goes)(copy.start)
    for copy, goes, _, _ in first:
        pl.when(goes)(copy.wait_send)
    for copy, goes, comes in second:
        pl.when(goes)(copy.wait_send)
        pl.when(comes)(copy.wait_recv)


def grads_kernel(sizes, factor, pattern, active, q, do, k, v, ld, dqa, dka, dva, pairs, dq, dk, dv):
    count = list_pairs(sizes, pattern, active, pairs)

    def clear(tile, carried):
        dq[tile] = jnp.zeros(dq.shape[1:], F32)

        @pl.when(tile < 6)
        def _():
            dk[tile] = jnp.zeros(dk.shape[1:], F32)
            dv[tile] = jnp.zeros(dv.shape[1:], F32)

        return carried

    lax.fori_loop(0, 12, clear, 0)

    def some(group, carried):
        spots = [pair_at(pairs, count, group * TOGETHER + x) for x in range(TOGETHER)]
        scores = [dot(k[key], q[query], NT) for key, query, _, _ in spots]
        slopes = [dot(v[key], do[query], NT) for key, query, _, _ in spots]
        probs = [jnp.exp2(x * factor - ld[query, 0:1, :]) for x, (_, query, _, _) in zip(scores, spots)]
        grads = [p * (x - ld[query, 1:2, :]) for p, x, (_, query, _, _) in zip(probs, slopes, spots)]
        probs = [x.astype(BF16) for x in probs]
        grads = [x.astype(BF16) for x in grads]
        values = [dot(x, do[query], NN) for x, (_, query, _, _) in zip(probs, spots)]
        keys = [dot(x, q[query], NN) for x, (_, query, _, _) in zip(grads, spots)]
        queries = [dot(k[key], x, TN) for x, (key, _, _, _) in zip(grads, spots)]
        for (_, _, key, query), x, y, z in zip(spots, queries, keys, values):
            dq[query] += x
            dk[key] += y
            dv[key] += z
        return carried

    lax.fori_loop(0, pl.cdiv(count, TOGETHER), some, 0)

    def finish(tile, carried):
        dqa[tile] = dq[tile].astype(BF16)

        @pl.when(tile < 6)
        def _():
            dka[tile] = dk[tile].astype(BF16)
            dva[tile] = dv[tile].astype(BF16)

        return carried

    lax.fori_loop(0, 12, finish, 0)


def return_kernel(
    sizes, scale, dqa, dka, dva, dq, dk, dv, time_in, key_in, value_in, edge, width_in, send_sem, recv_sem
):
    links = Links(sizes, send_sem, recv_sem)
    there = links.there
    links.greet([W_UP, W_DOWN, T_UP, T_DOWN, H_UP, H_DOWN])
    copies = []
    for number, (src, dst, step) in enumerate(
        (
            (dqa.at[2], time_in.at[0], T_UP),
            (dqa.at[0], time_in.at[1], T_DOWN),
            (dka.at[2], key_in.at[0], H_UP),
            (dka.at[0], key_in.at[1], H_DOWN),
            (dva.at[2], value_in.at[0], H_UP),
            (dva.at[0], value_in.at[1], H_DOWN),
        )
    ):
        copy = links.copy(src, dst, number, step)
        pl.when(there(step))(copy.start)
        copies.append((copy, step, dst))
    edges = []
    for number, (src, dst, step) in enumerate(
        ((edge.at[1], width_in.at[0], W_UP), (edge.at[0], width_in.at[1], W_DOWN))
    ):
        edges.append((links.copy(src, dst, 6 + number, step), step, dst))

    def take(entry):
        copy, step, dst = entry
        comes = there(back(step))

        @pl.when(jnp.logical_not(comes))
        def _():
            dst[...] = jnp.zeros(dst.shape, dst.dtype)

        pl.when(comes)(copy.wait_recv)

    take(copies[0])
    take(copies[1])
    for spot, column in ((0, 0), (1, 3)):
        total = dqa[1, column].astype(F32) + time_in[0, column].astype(F32) + time_in[1, column].astype(F32)
        edge[spot] = total.astype(BF16)
    for copy, step, _ in edges:
        pl.when(there(step))(copy.start)
    for entry in copies[2:]:
        take(entry)
    for tile in range(2):
        total = dka[1, tile].astype(F32) + key_in[0, tile].astype(F32) + key_in[1, tile].astype(F32)
        dk[tile] = (total * scale).astype(BF16)
        total = dva[1, tile].astype(F32) + value_in[0, tile].astype(F32) + value_in[1, tile].astype(F32)
        dv[tile] = total.astype(BF16)
    for entry in edges:
        take(entry)
    for tile in range(2):
        total = dqa[1, 1 + tile].astype(F32) + width_in[tile].astype(F32)
        total = total + time_in[0, 1 + tile].astype(F32) + time_in[1, 1 + tile].astype(F32)
        dq[tile] = (total * scale).T.astype(BF16)
    for copy, step, _ in copies + edges:
        pl.when(there(step))(copy.wait_send)


def params(number=None, megabytes=40):
    if number is None:
        return pltpu.CompilerParams(vmem_limit_bytes=megabytes << 20)
    return pltpu.CompilerParams(
        collective_id=number, has_side_effects=True, vmem_limit_bytes=megabytes << 20
    )


def shape(*dims, dtype=BF16):
    return jax.ShapeDtypeStruct(dims, dtype)


def on_device(sizes, queries, key_tiles, value_tiles, forward_out, out_grad, pattern, tile_active):
    whole = queries.shape
    tile, feat = whole[4], whole[5]
    scale = 1.0 / math.sqrt(feat)
    factor = scale * math.log2(math.e)
    q, k, v, fo, do = (
        x.reshape(2, tile, feat) for x in (queries, key_tiles, value_tiles, forward_out, out_grad)
    )
    active = tile_active.reshape(-1, tile_active.shape[2])
    hbm = pl.BlockSpec(memory_space=pl.ANY)
    vmem = pl.BlockSpec(memory_space=pltpu.VMEM)
    smem = pl.BlockSpec(memory_space=pltpu.SMEM)
    dma = pltpu.SemaphoreType.DMA

    qa, doa, ka, va = pl.pallas_call(
        functools.partial(gather_kernel, sizes),
        out_shape=[
            shape(3, 4, tile, feat),
            shape(3, 4, tile, feat),
            shape(3, 2, tile, feat),
            shape(3, 2, tile, feat),
        ],
        in_specs=[hbm] * 4,
        out_specs=[hbm] * 4,
        scratch_shapes=[dma((4,)), dma((20,)), dma((20,))],
        compiler_params=params(0),
        name="gather",
    )(q, do, k, v)
    qa, doa = (x.reshape(12, tile, feat) for x in (qa, doa))
    ka, va = (x.reshape(6, tile, feat) for x in (ka, va))

    part = pl.pallas_call(
        functools.partial(stats_kernel, sizes, factor),
        out_shape=shape(12, 8, tile, dtype=F32),
        in_specs=[smem, smem, vmem, vmem, vmem, vmem],
        out_specs=vmem,
        scratch_shapes=[pltpu.SMEM((64,), jnp.int32), pltpu.VMEM((13, 8, tile), F32)],
        compiler_params=params(),
        name="stats",
    )(pattern, active, qa, ka, do, fo)

    ld = pl.pallas_call(
        functools.partial(totals_kernel, sizes),
        out_shape=shape(3, 4, 8, tile, dtype=F32),
        in_specs=[vmem],
        out_specs=vmem,
        scratch_shapes=[pltpu.VMEM((8, 2, 8, tile), F32), dma((16,)), dma((16,))],
        compiler_params=params(1),
        name="totals",
    )(part.reshape(3, 4, 8, tile))

    dqa, dka, dva = pl.pallas_call(
        functools.partial(grads_kernel, sizes, factor),
        out_shape=[shape(12, feat, tile), shape(6, tile, feat), shape(6, tile, feat)],
        in_specs=[smem, smem, vmem, vmem, vmem, vmem, vmem],
        out_specs=[vmem] * 3,
        scratch_shapes=[
            pltpu.SMEM((64,), jnp.int32),
            pltpu.VMEM((13, feat, tile), F32),
            pltpu.VMEM((7, tile, feat), F32),
            pltpu.VMEM((7, tile, feat), F32),
        ],
        compiler_params=params(),
        name="grads",
    )(pattern, active, qa, doa, ka, va, ld.reshape(12, 8, tile))

    dq, dk, dv = pl.pallas_call(
        functools.partial(return_kernel, sizes, scale),
        out_shape=[shape(2, tile, feat)] * 3,
        in_specs=[vmem] * 3,
        out_specs=[vmem] * 3,
        scratch_shapes=[
            pltpu.VMEM((2, 4, feat, tile), BF16),
            pltpu.VMEM((2, 2, tile, feat), BF16),
            pltpu.VMEM((2, 2, tile, feat), BF16),
            pltpu.VMEM((2, feat, tile), BF16),
            pltpu.VMEM((2, feat, tile), BF16),
            dma((8,)),
            dma((8,)),
        ],
        compiler_params=params(2),
        name="returns",
    )(dqa.reshape(3, 4, feat, tile), dka.reshape(3, 2, tile, feat), dva.reshape(3, 2, tile, feat))
    return dq.reshape(whole), dk.reshape(whole), dv.reshape(whole)


def solution(mesh):
    tiles = P("ta", "ha", "wa", None, None, None)
    sizes = tuple(mesh.shape[axis] for axis in ("ta", "ha", "wa"))
    return jax.shard_map(
        functools.partial(on_device, sizes),
        mesh=mesh,
        in_specs=(tiles,) * 5 + (P(), P()),
        out_specs=(tiles,) * 3,
        check_vma=False,
    )
```

```python
import functools
import math

import jax
import jax.numpy as jnp
from jax import lax
from jax.experimental import pallas as pl
from jax.experimental.pallas import tpu as pltpu
from jax.sharding import PartitionSpec as P

MESH = pl.DeviceIdType.MESH
F32 = jnp.float32
BF16 = jnp.bfloat16
NT = (((1,), (1,)), ((), ()))
TN = (((0,), (0,)), ((), ()))
NN = (((1,), (0,)), ((), ()))
LOW = -1e30
TOGETHER = 3


def dot(left, right, form):
    return lax.dot_general(left, right, form, preferred_element_type=F32)


def position():
    return lax.axis_index("ta"), lax.axis_index("ha"), lax.axis_index("wa")


class Links:
    def __init__(self, sizes, send_sem, recv_sem):
        self.sizes = sizes
        self.at = position()
        self.send_sem = send_sem
        self.recv_sem = recv_sem

    def there(self, step):
        found = None
        for place, size, by in zip(self.at, self.sizes, step):
            if by:
                ok = (place + by >= 0) & (place + by < size)
                found = ok if found is None else found & ok
        return found

    def device(self, step):
        return tuple(
            lax.rem(place + by + size, size) for place, size, by in zip(self.at, self.sizes, step)
        )

    def greet(self, steps):
        barrier = pltpu.get_barrier_semaphore()
        count = 0
        for step in steps:
            count = count + self.there(step).astype(jnp.int32)

            @pl.when(self.there(step))
            def _():
                pl.semaphore_signal(
                    barrier, inc=1, device_id=self.device(step), device_id_type=MESH
                )

        pl.semaphore_wait(barrier, count)

    def copy(self, src, dst, number, step):
        return pltpu.make_async_remote_copy(
            src_ref=src,
            dst_ref=dst,
            send_sem=self.send_sem.at[number],
            recv_sem=self.recv_sem.at[number],
            device_id=self.device(step),
            device_id_type=MESH,
        )


def back(step):
    return tuple(-by for by in step)


W_UP, W_DOWN, T_UP, T_DOWN, H_UP, H_DOWN = (
    (0, 0, 1),
    (0, 0, -1),
    (1, 0, 0),
    (-1, 0, 0),
    (0, 1, 0),
    (0, -1, 0),
)


def all_there(*conditions):
    return functools.reduce(jnp.logical_and, conditions)


PLANE = [(dt, dw) for dt in (-1, 0, 1) for dw in (-1, 0, 1) if (dt, dw) != (0, 0)]
WIDE = [(dt, dw) for dt in (-2, -1, 0, 1, 2) for dw in (-1, 0, 1) if (dt, dw) != (0, 0)]


def side_of(dw):
    return dw % 3


def meet_kernel(
    sizes, factor, pattern, active, q, do, k, v, fo, qa, doa, ka, va, inbox, dots, own_fo, local_sem, send_sem, recv_sem
):
    links = Links(sizes, send_sem, recv_sem)
    there = links.there
    t, h, w = links.at
    nt, nh, nw = sizes
    tile = q.shape[1]
    row_in = [t > 0, t >= 0, t < nt - 1]

    stay = [
        pltpu.make_async_copy(src, dst, local_sem.at[spot])
        for spot, (src, dst) in enumerate(
            (
                (do, doa.at[1, pl.ds(1, 2)]),
                (fo, own_fo),
                (q, qa.at[1, pl.ds(1, 2)]),
                (k, ka.at[1]),
                (v, va.at[1]),
            )
        )
    ]
    for copy in stay:
        copy.start()
    links.greet([(dt, 0, dw) for dt, dw in WIDE] + [H_UP, H_DOWN])

    groups = []
    number = 0
    for rows, rows_all, cols, cols_all in ((q, qa, k, ka), (do, doa, v, va)):
        width = [
            (links.copy(rows.at[1], rows_all.at[1, 0], number, W_UP), there(W_UP), there(W_DOWN)),
            (links.copy(rows.at[0], rows_all.at[1, 3], number + 1, W_DOWN), there(W_DOWN), there(W_UP)),
        ]
        time = [
            (links.copy(rows, rows_all.at[0, pl.ds(1, 2)], number + 2, T_UP), there(T_UP), there(T_DOWN)),
            (links.copy(rows, rows_all.at[2, pl.ds(1, 2)], number + 3, T_DOWN), there(T_DOWN), there(T_UP)),
        ]
        height = [
            (links.copy(cols, cols_all.at[0], number + 4, H_UP), there(H_UP), there(H_DOWN)),
            (links.copy(cols, cols_all.at[2], number + 5, H_DOWN), there(H_DOWN), there(H_UP)),
        ]
        number += 6
        fans = []
        for spot, has in ((0, there(W_DOWN)), (3, there(W_UP))):
            for step, slot in ((T_UP, 0), (T_DOWN, 2)):
                fan = links.copy(rows_all.at[1, spot], rows_all.at[slot, spot], number, step)
                fans.append((fan, has & there(step), has & there(back(step)), slot))
                number += 1
        groups.append((width, time, height, fans))
    for width, time, height, _ in groups:
        for copy, goes, _ in width + time + height:
            pl.when(goes)(copy.start)

    stay[0].wait()
    stay[1].wait()
    dots[1, 0] = jnp.zeros(dots.shape[2:], F32)
    for spot in range(2):
        both = doa[1, 1 + spot].astype(F32) * own_fo[spot].astype(F32)
        dots[1, 0, spot : spot + 1, :] = jnp.sum(both.T, axis=0, keepdims=True)
    small = []
    for dt, dw in PLANE:
        step = (dt, 0, dw)
        copy = links.copy(dots.at[1, 0], dots.at[1 - dt, side_of(dw)], number, step)
        number += 1
        pl.when(there(step))(copy.start)
        small.append((copy, there(step), there(back(step))))

    def arrive(entries):
        for copy, _, comes in entries:
            pl.when(comes)(copy.wait_recv)

    def forward(group):
        width, _, _, fans = group
        arrive(width)
        for fan, goes, _, _ in fans:
            pl.when(goes)(fan.start)

    def lit(row, col):
        key_h = h + row - 1
        inside = (key_h >= 0) & (key_h < nh)
        spot = t * nh + jnp.clip(key_h, 0, nh - 1)
        return inside, inside & (active[spot, 2 * w + col] == 1)

    def totals(time, row, carried):
        top, total = carried
        tops = [[top[x : x + 1]] for x in range(4)]
        scores = []
        oks = []
        for col in range(2):
            inside, on = lit(row, col)
            x = dot(ka[row, col], qa[time, pl.ds(col, 3)].reshape(3 * tile, -1), NT) * factor
            high = jnp.max(x, axis=0, keepdims=True)
            scores.append(x)
            for shift in range(3):
                offset = 9 * (2 - time) + 3 * row + 2 - shift
                ok = (on & (pattern[0, offset] == 1)) | (inside & (offset == 13))
                tops[col + shift].append(jnp.where(ok, high[:, shift * tile : (shift + 1) * tile], LOW))
                oks.append(ok)
        tops = [functools.reduce(jnp.maximum, x) for x in tops]
        sums = [total[x : x + 1] * jnp.exp2(top[x : x + 1] - tops[x]) for x in range(4)]
        for col in range(2):
            part = jnp.exp2(scores[col] - jnp.concatenate(tops[col : col + 3], axis=1))
            part = jnp.sum(part, axis=0, keepdims=True)
            for shift in range(3):
                term = jnp.where(oks[3 * col + shift], part[:, shift * tile : (shift + 1) * tile], 0.0)
                sums[col + shift] = sums[col + shift] + term
        return jnp.concatenate(tops, axis=0), jnp.concatenate(sums, axis=0)

    fresh = (jnp.full((4, tile), LOW, F32), jnp.zeros((4, tile), F32))

    def publish(time, carried):
        nonlocal number
        inbox[time, time, 0, 0:4, :], inbox[time, time, 0, 4:8, :] = carried
        for dt in (time - 2, time - 1, time):
            for dw in (-1, 0, 1):
                if (dt, dw) == (0, 0):
                    continue
                step = (dt, 0, dw)
                slot = inbox.at[time - dt, time, side_of(dw)]
                copy = links.copy(inbox.at[time, time, 0], slot, number, step)
                number += 1
                goes = row_in[time] & there(step)
                pl.when(goes)(copy.start)
                small.append((copy, goes, row_in[time - dt] & there(back(step))))

    stay[2].wait()
    stay[3].wait()
    forward(groups[0])
    carried = totals(1, 1, fresh)
    arrive(groups[0][2])
    carried = lax.fori_loop(0, 2, lambda x, c: totals(1, 2 * x, c), carried)
    publish(1, carried)
    forward(groups[1])
    for time, entry in ((0, 0), (2, 1)):
        arrive([groups[0][1][entry]])
        arrive([fan[:3] for fan in groups[0][3] if fan[3] == time])
        publish(time, lax.fori_loop(0, 3, lambda x, c: totals(time, x, c), fresh))

    arrive(groups[1][1] + groups[1][2] + [fan[:3] for fan in groups[1][3]] + small)
    stay[4].wait()
    for width, time, height, fans in groups:
        for copy, goes, _ in width + time + height + [fan[:3] for fan in fans]:
            pl.when(goes)(copy.wait_send)
    for copy, goes, _ in small:
        pl.when(goes)(copy.wait_send)


def list_pairs(sizes, pattern, active, pairs):
    t, h, w = position()
    nt, nh, nw = sizes

    def keys(place, count):
        row, col = place // 2, place % 2
        key_in = (h + row - 1 >= 0) & (h + row - 1 < nh)
        key_h = jnp.clip(h + row - 1, 0, nh - 1)
        lit = active[t * nh + key_h, 2 * w + col]
        for time in range(3):
            time_in = (t + time - 1 >= 0) & (t + time - 1 < nt)
            for shift in range(3):
                spot = col + 2 - shift
                inside = key_in & time_in & (2 * w + spot - 1 >= 0) & (2 * w + spot - 1 < 2 * nw)
                offset = 9 * (2 - time) + 3 * row + shift
                chosen = (pattern[0, offset] == 1) & (lit == 1)
                pairs[count] = place * 12 + time * 4 + spot
                count = count + (inside & (chosen | (offset == 13))).astype(jnp.int32)
        return count

    return lax.fori_loop(0, 6, keys, jnp.int32(0))


def pair_at(pairs, count, index):
    real = index < count
    code = jnp.where(real, pairs[jnp.minimum(index, count - 1)], 0)
    key, query = code // 12, code % 12
    return key, query, jnp.where(real, key, 6), jnp.where(real, query, 12)


def join_totals(sizes, inbox, dots, ld):
    t, h, w = position()
    for time in range(3):
        terms = []
        for sender in range(3):
            ok = (t + time - sender >= 0) & (t + time - sender < sizes[0])
            left, right = ok & (w > 0), ok & (w < sizes[2] - 1)
            parts = [(inbox[time, sender, 0], ok, ok)]
            parts.append(
                (
                    jnp.concatenate(
                        [
                            inbox[time, sender, 1, 2:4, :],
                            inbox[time, sender, 2, 0:2, :],
                            inbox[time, sender, 1, 6:8, :],
                            inbox[time, sender, 2, 4:6, :],
                        ],
                        axis=0,
                    ),
                    left,
                    right,
                )
            )
            for both, first, last in parts:
                good = jnp.concatenate(
                    [jnp.full((2, both.shape[1]), x.astype(jnp.int32)) for x in (first, last)], axis=0
                )
                terms.append(
                    (jnp.where(good == 1, both[0:4], LOW), jnp.where(good == 1, both[4:8], 0.0))
                )
        top = functools.reduce(jnp.maximum, [x for x, _ in terms])
        total = sum(y * jnp.exp2(x - top) for x, y in terms)
        total = top + jnp.log2(total)
        for spot, (side, line) in enumerate(((1, 1), (0, 0), (0, 1), (2, 0))):
            ld[4 * time + spot, 0:1, :] = total[spot : spot + 1]
            ld[4 * time + spot, 1:2, :] = dots[time, side, line : line + 1, :]


def grads_kernel(
    sizes, factor, pattern, active, q, do, k, v, inbox, dots, dqa, dka, dva, pairs, ld, dq, dk, dv
):
    count = list_pairs(sizes, pattern, active, pairs)
    join_totals(sizes, inbox, dots, ld)

    def clear(tile, carried):
        dq[tile] = jnp.zeros(dq.shape[1:], F32)

        @pl.when(tile < 6)
        def _():
            dk[tile] = jnp.zeros(dk.shape[1:], F32)
            dv[tile] = jnp.zeros(dv.shape[1:], F32)

        return carried

    lax.fori_loop(0, 12, clear, 0)

    def some(group, carried):
        spots = [pair_at(pairs, count, group * TOGETHER + x) for x in range(TOGETHER)]
        scores = [dot(k[key], q[query], NT) for key, query, _, _ in spots]
        slopes = [dot(v[key], do[query], NT) for key, query, _, _ in spots]
        probs = [jnp.exp2(x * factor - ld[query, 0:1, :]) for x, (_, query, _, _) in zip(scores, spots)]
        grads = [p * (x - ld[query, 1:2, :]) for p, x, (_, query, _, _) in zip(probs, slopes, spots)]
        probs = [x.astype(BF16) for x in probs]
        grads = [x.astype(BF16) for x in grads]
        values = [dot(x, do[query], NN) for x, (_, query, _, _) in zip(probs, spots)]
        keys = [dot(x, q[query], NN) for x, (_, query, _, _) in zip(grads, spots)]
        queries = [dot(k[key], x, TN) for x, (key, _, _, _) in zip(grads, spots)]
        for (_, _, key, query), x, y, z in zip(spots, queries, keys, values):
            dq[query] += x
            dk[key] += y
            dv[key] += z
        return carried

    lax.fori_loop(0, pl.cdiv(count, TOGETHER), some, 0)

    def finish(tile, carried):
        dqa[tile] = dq[tile].astype(BF16)

        @pl.when(tile < 6)
        def _():
            dka[tile] = dk[tile].astype(BF16)
            dva[tile] = dv[tile].astype(BF16)

        return carried

    lax.fori_loop(0, 12, finish, 0)


def return_kernel(
    sizes, scale, dqa, dka, dva, dq, dk, dv, time_in, key_in, value_in, edge, width_in, send_sem, recv_sem
):
    links = Links(sizes, send_sem, recv_sem)
    there = links.there
    links.greet([W_UP, W_DOWN, T_UP, T_DOWN, H_UP, H_DOWN])
    copies = []
    for number, (src, dst, step) in enumerate(
        (
            (dqa.at[2], time_in.at[0], T_UP),
            (dqa.at[0], time_in.at[1], T_DOWN),
            (dka.at[2], key_in.at[0], H_UP),
            (dka.at[0], key_in.at[1], H_DOWN),
            (dva.at[2], value_in.at[0], H_UP),
            (dva.at[0], value_in.at[1], H_DOWN),
        )
    ):
        copy = links.copy(src, dst, number, step)
        pl.when(there(step))(copy.start)
        copies.append((copy, step, dst))
    edges = []
    for number, (src, dst, step) in enumerate(
        ((edge.at[1], width_in.at[0], W_UP), (edge.at[0], width_in.at[1], W_DOWN))
    ):
        edges.append((links.copy(src, dst, 6 + number, step), step, dst))

    def take(entry):
        copy, step, dst = entry
        comes = there(back(step))

        @pl.when(jnp.logical_not(comes))
        def _():
            dst[...] = jnp.zeros(dst.shape, dst.dtype)

        pl.when(comes)(copy.wait_recv)

    take(copies[0])
    take(copies[1])
    for spot, column in ((0, 0), (1, 3)):
        total = dqa[1, column].astype(F32) + time_in[0, column].astype(F32) + time_in[1, column].astype(F32)
        edge[spot] = total.astype(BF16)
    for copy, step, _ in edges:
        pl.when(there(step))(copy.start)
    for entry in copies[2:]:
        take(entry)
    for tile in range(2):
        total = dka[1, tile].astype(F32) + key_in[0, tile].astype(F32) + key_in[1, tile].astype(F32)
        dk[tile] = (total * scale).astype(BF16)
        total = dva[1, tile].astype(F32) + value_in[0, tile].astype(F32) + value_in[1, tile].astype(F32)
        dv[tile] = total.astype(BF16)
    for entry in edges:
        take(entry)
    for tile in range(2):
        total = dqa[1, 1 + tile].astype(F32) + width_in[tile].astype(F32)
        total = total + time_in[0, 1 + tile].astype(F32) + time_in[1, 1 + tile].astype(F32)
        dq[tile] = (total * scale).T.astype(BF16)
    for copy, step, _ in copies + edges:
        pl.when(there(step))(copy.wait_send)


def params(number=None, megabytes=40):
    if number is None:
        return pltpu.CompilerParams(vmem_limit_bytes=megabytes << 20)
    return pltpu.CompilerParams(
        collective_id=number, has_side_effects=True, vmem_limit_bytes=megabytes << 20
    )


def shape(*dims, dtype=BF16):
    return jax.ShapeDtypeStruct(dims, dtype)


def on_device(sizes, queries, key_tiles, value_tiles, forward_out, out_grad, pattern, tile_active):
    whole = queries.shape
    tile, feat = whole[4], whole[5]
    scale = 1.0 / math.sqrt(feat)
    factor = scale * math.log2(math.e)
    q, k, v, fo, do = (
        x.reshape(2, tile, feat) for x in (queries, key_tiles, value_tiles, forward_out, out_grad)
    )
    active = tile_active.reshape(-1, tile_active.shape[2])
    hbm = pl.BlockSpec(memory_space=pltpu.HBM)
    vmem = pl.BlockSpec(memory_space=pltpu.VMEM)
    smem = pl.BlockSpec(memory_space=pltpu.SMEM)
    dma = pltpu.SemaphoreType.DMA

    qa, doa, ka, va, inbox, dots = pl.pallas_call(
        functools.partial(meet_kernel, sizes, factor),
        out_shape=[
            shape(3, 4, tile, feat),
            shape(3, 4, tile, feat),
            shape(3, 2, tile, feat),
            shape(3, 2, tile, feat),
            shape(3, 3, 3, 8, tile, dtype=F32),
            shape(3, 3, 8, tile, dtype=F32),
        ],
        in_specs=[smem] * 2 + [hbm] * 5,
        out_specs=[vmem] * 6,
        scratch_shapes=[pltpu.VMEM((2, tile, feat), BF16), dma((5,)), dma((52,)), dma((52,))],
        compiler_params=params(0),
        name="meet",
    )(pattern, active, q, do, k, v, fo)
    qa, doa = (x.reshape(12, tile, feat) for x in (qa, doa))
    ka, va = (x.reshape(6, tile, feat) for x in (ka, va))

    dqa, dka, dva = pl.pallas_call(
        functools.partial(grads_kernel, sizes, factor),
        out_shape=[shape(12, feat, tile), shape(6, tile, feat), shape(6, tile, feat)],
        in_specs=[smem] * 2 + [vmem] * 6,
        out_specs=[vmem] * 3,
        scratch_shapes=[
            pltpu.SMEM((64,), jnp.int32),
            pltpu.VMEM((12, 8, tile), F32),
            pltpu.VMEM((13, feat, tile), F32),
            pltpu.VMEM((7, tile, feat), F32),
            pltpu.VMEM((7, tile, feat), F32),
        ],
        compiler_params=params(),
        name="grads",
    )(pattern, active, qa, doa, ka, va, inbox, dots)

    dq, dk, dv = pl.pallas_call(
        functools.partial(return_kernel, sizes, scale),
        out_shape=[shape(2, tile, feat)] * 3,
        in_specs=[vmem] * 3,
        out_specs=[vmem] * 3,
        scratch_shapes=[
            pltpu.VMEM((2, 4, feat, tile), BF16),
            pltpu.VMEM((2, 2, tile, feat), BF16),
            pltpu.VMEM((2, 2, tile, feat), BF16),
            pltpu.VMEM((2, feat, tile), BF16),
            pltpu.VMEM((2, feat, tile), BF16),
            dma((8,)),
            dma((8,)),
        ],
        compiler_params=params(1),
        name="returns",
    )(dqa.reshape(3, 4, feat, tile), dka.reshape(3, 2, tile, feat), dva.reshape(3, 2, tile, feat))
    return dq.reshape(whole), dk.reshape(whole), dv.reshape(whole)


def solution(mesh):
    tiles = P("ta", "ha", "wa", None, None, None)
    sizes = tuple(mesh.shape[axis] for axis in ("ta", "ha", "wa"))
    return jax.shard_map(
        functools.partial(on_device, sizes),
        mesh=mesh,
        in_specs=(tiles,) * 5 + (P(), P()),
        out_specs=(tiles,) * 3,
        check_vma=False,
    )
```

```python
import functools
import math

import jax
import jax.numpy as jnp
from jax import lax
from jax.experimental import pallas as pl
from jax.experimental.pallas import tpu as pltpu
from jax.sharding import PartitionSpec as P

MESH = pl.DeviceIdType.MESH
F32 = jnp.float32
BF16 = jnp.bfloat16
NT = (((1,), (1,)), ((), ()))
TN = (((0,), (0,)), ((), ()))
NN = (((1,), (0,)), ((), ()))
LOW = -1e30


def dot(left, right, form):
    return lax.dot_general(left, right, form, preferred_element_type=F32)


def position():
    return lax.axis_index("ta"), lax.axis_index("ha"), lax.axis_index("wa")


class Links:
    def __init__(self, sizes, send_sem, recv_sem):
        self.sizes = sizes
        self.at = position()
        self.send_sem = send_sem
        self.recv_sem = recv_sem

    def there(self, step):
        found = None
        for place, size, by in zip(self.at, self.sizes, step):
            if by:
                ok = (place + by >= 0) & (place + by < size)
                found = ok if found is None else found & ok
        return found

    def device(self, step):
        return tuple(
            lax.rem(place + by + size, size) for place, size, by in zip(self.at, self.sizes, step)
        )

    def greet(self, steps):
        barrier = pltpu.get_barrier_semaphore()
        count = 0
        for step in steps:
            count = count + self.there(step).astype(jnp.int32)

            @pl.when(self.there(step))
            def _():
                pl.semaphore_signal(
                    barrier, inc=1, device_id=self.device(step), device_id_type=MESH
                )

        pl.semaphore_wait(barrier, count)

    def copy(self, src, dst, number, step):
        return pltpu.make_async_remote_copy(
            src_ref=src,
            dst_ref=dst,
            send_sem=self.send_sem.at[number],
            recv_sem=self.recv_sem.at[number],
            device_id=self.device(step),
            device_id_type=MESH,
        )


def back(step):
    return tuple(-by for by in step)


W_UP, W_DOWN, T_UP, T_DOWN, H_UP, H_DOWN = (
    (0, 0, 1),
    (0, 0, -1),
    (1, 0, 0),
    (-1, 0, 0),
    (0, 1, 0),
    (0, -1, 0),
)


def all_there(*conditions):
    return functools.reduce(jnp.logical_and, conditions)


PLANE = [(dt, dw) for dt in (-1, 0, 1) for dw in (-1, 0, 1) if (dt, dw) != (0, 0)]
WIDE = [(dt, dw) for dt in (-2, -1, 0, 1, 2) for dw in (-1, 0, 1) if (dt, dw) != (0, 0)]


def side_of(dw):
    return dw % 3


PAIRS = [(col, shift) for col in range(2) for shift in range(3)]


def attend_kernel(
    sizes, scale, pattern, active, q, do, k, v, fo, out_dq, out_dk, out_dv,
    qa, doa, ka, va, own_fo, inbox, dots, tops, sums, raised, dq, dk, dv,
    send_q, send_k, send_v, time_in, key_in, value_in, edge, width_in, local_sem, send_sem, recv_sem,
):
    links = Links(sizes, send_sem, recv_sem)
    there = links.there
    t, h, w = links.at
    nt, nh, nw = sizes
    tile = q.shape[1]
    factor = scale * math.log2(math.e)
    row_in = [t > 0, t >= 0, t < nt - 1]
    col_in = [w > 0, w >= 0, w >= 0, w < nw - 1]

    stay = [
        pltpu.make_async_copy(src, dst, local_sem.at[spot])
        for spot, (src, dst) in enumerate(
            (
                (do, doa.at[1, pl.ds(1, 2)]),
                (fo, own_fo),
                (q, qa.at[1, pl.ds(1, 2)]),
                (k, ka.at[1]),
                (v, va.at[1]),
            )
        )
    ]
    for copy in stay:
        copy.start()
    links.greet([(dt, 0, dw) for dt, dw in WIDE] + [H_UP, H_DOWN])

    groups = []
    number = 0
    for rows, rows_all, cols, cols_all in ((q, qa, k, ka), (do, doa, v, va)):
        width = [
            (links.copy(rows.at[1], rows_all.at[1, 0], number, W_UP), there(W_UP), there(W_DOWN)),
            (links.copy(rows.at[0], rows_all.at[1, 3], number + 1, W_DOWN), there(W_DOWN), there(W_UP)),
        ]
        time = [
            (links.copy(rows, rows_all.at[0, pl.ds(1, 2)], number + 2, T_UP), there(T_UP), there(T_DOWN)),
            (links.copy(rows, rows_all.at[2, pl.ds(1, 2)], number + 3, T_DOWN), there(T_DOWN), there(T_UP)),
        ]
        height = [
            (links.copy(cols, cols_all.at[0], number + 4, H_UP), there(H_UP), there(H_DOWN)),
            (links.copy(cols, cols_all.at[2], number + 5, H_DOWN), there(H_DOWN), there(H_UP)),
        ]
        number += 6
        fans = []
        for spot, has in ((0, there(W_DOWN)), (3, there(W_UP))):
            for step, slot in ((T_UP, 0), (T_DOWN, 2)):
                fan = links.copy(rows_all.at[1, spot], rows_all.at[slot, spot], number, step)
                fans.append((fan, has & there(step), has & there(back(step)), slot))
                number += 1
        groups.append((width, time, height, fans))

    def send(group):
        width, time, height, _ = group
        for copy, goes, _ in width + time + height:
            pl.when(goes)(copy.start)

    def arrive(entries):
        for copy, _, comes in entries:
            pl.when(comes)(copy.wait_recv)

    def forward(group):
        width, _, _, fans = group
        arrive(width)
        for fan, goes, _, _ in fans:
            pl.when(goes)(fan.start)

    send(groups[0])
    stay[0].wait()
    stay[1].wait()
    dots[1, 0] = jnp.zeros(dots.shape[2:], F32)
    for spot in range(2):
        both = doa[1, 1 + spot].astype(F32) * own_fo[spot].astype(F32)
        dots[1, 0, spot : spot + 1, :] = jnp.sum(both.T, axis=0, keepdims=True)
    small = []
    for dt, dw in PLANE:
        step = (dt, 0, dw)
        copy = links.copy(dots.at[1, 0], dots.at[1 - dt, side_of(dw)], number, step)
        number += 1
        pl.when(there(step))(copy.start)
        small.append((copy, there(step), there(back(step))))

    def clear(ref, *spot):
        ref[spot] = jnp.zeros(ref.shape[len(spot) :], ref.dtype)

    def clear_sums(x, carried):
        for y in range(4):
            clear(dq, x, y)
        for y in range(2):
            clear(dk, x, y)
            clear(dv, x, y)
        return carried

    lax.fori_loop(0, 3, clear_sums, 0)
    for time in range(3):
        for spot in range(4):
            if (time, spot) not in ((1, 1), (1, 2)):

                @pl.when(jnp.logical_not(row_in[time] & col_in[spot]))
                def _():
                    clear(qa, time, spot)
                    clear(doa, time, spot)

    for row, step in ((0, H_DOWN), (2, H_UP)):

        @pl.when(jnp.logical_not(there(step)))
        def _():
            clear(ka, row)
            clear(va, row)

    def allowed(time, row):
        key_h = h + row - 1
        key_in = (key_h >= 0) & (key_h < nh)
        line = t * nh + jnp.clip(key_h, 0, nh - 1)
        found = []
        for col, shift in PAIRS:
            offset = 9 * (2 - time) + 3 * row + 2 - shift
            on = (active[line, 2 * w + col] == 1) & (pattern[0, offset] == 1)
            inside = key_in & row_in[time] & col_in[col + shift]
            found.append(inside & (on | (offset == 13)))
        return found

    def window(ref, time, col):
        return ref[time, pl.ds(col, 3)].reshape(3 * tile, -1)

    def raise_scores(time, row):
        for col in range(2):
            x = dot(ka[row, col], window(qa, time, col), NT) * factor
            high = jnp.max(x, axis=0, keepdims=True)
            x = jnp.exp2(x - high)
            raised[time, row, col] = x.astype(BF16)
            total = jnp.sum(x, axis=0, keepdims=True)
            for shift in range(3):
                spot = slice(shift * tile, (shift + 1) * tile)
                tops[time, row, 3 * col + shift : 3 * col + shift + 1, :] = high[:, spot]
                sums[time, row, 3 * col + shift : 3 * col + shift + 1, :] = total[:, spot]

    def publish(time):
        nonlocal number
        terms = [[] for _ in range(4)]
        for row in range(3):
            for x, ((col, shift), ok) in enumerate(zip(PAIRS, allowed(time, row))):
                high = jnp.where(ok, tops[time, row, x : x + 1, :], LOW)
                terms[col + shift].append((high, jnp.where(ok, sums[time, row, x : x + 1, :], 0.0)))
        for spot in range(4):
            top = functools.reduce(jnp.maximum, [x for x, _ in terms[spot]])
            inbox[time, time, 0, spot : spot + 1, :] = top
            total = sum(y * jnp.exp2(x - top) for x, y in terms[spot])
            inbox[time, time, 0, 4 + spot : 5 + spot, :] = total
        for dt in (time - 2, time - 1, time):
            for dw in (-1, 0, 1):
                if (dt, dw) == (0, 0):
                    continue
                step = (dt, 0, dw)
                slot = inbox.at[time - dt, time, side_of(dw)]
                copy = links.copy(inbox.at[time, time, 0], slot, number, step)
                number += 1
                goes = row_in[time] & there(step)
                pl.when(goes)(copy.start)
                small.append((copy, goes, row_in[time - dt] & there(back(step))))

    def each(first, last, act):
        def step(x, carried):
            act(x)
            return carried

        lax.fori_loop(first, last, step, 0)

    stay[2].wait()
    stay[3].wait()
    forward(groups[0])
    arrive(groups[0][2])
    send(groups[1])
    each(0, 3, lambda x: raise_scores(1, x))
    publish(1)
    forward(groups[1])
    arrive(groups[0][1])
    arrive([fan[:3] for fan in groups[0][3]])
    each(0, 3, lambda x: raise_scores(0, x))
    publish(0)
    each(0, 3, lambda x: raise_scores(2, x))
    publish(2)
    arrive(groups[1][1] + groups[1][2] + [fan[:3] for fan in groups[1][3]])
    stay[4].wait()
    arrive(small)

    for time in range(3):
        terms = []
        for sender in range(3):
            ok = (t + time - sender >= 0) & (t + time - sender < nt)
            for spot, sides in ((0, (0, 0)), (2, (1, 2))):
                lines = []
                for half, side in enumerate(sides):
                    good = ok if side == 0 else ok & (w > 0) if side == 1 else ok & (w < nw - 1)
                    first = 2 * half if side == 0 else 2 - 2 * half
                    lines.append(
                        (
                            jnp.where(good, inbox[time, sender, side, first : first + 2, :], LOW),
                            jnp.where(good, inbox[time, sender, side, 4 + first : 6 + first, :], 0.0),
                        )
                    )
                terms.append(tuple(jnp.concatenate(x, axis=0) for x in zip(*lines)))
        top = functools.reduce(jnp.maximum, [x for x, _ in terms])
        log_total = top + jnp.log2(sum(y * jnp.exp2(x - top) for x, y in terms))
        for row in range(3):
            for x, ((col, shift), ok) in enumerate(zip(PAIRS, allowed(time, row))):
                part = jnp.exp2(tops[time, row, x : x + 1, :] - log_total[col + shift : col + shift + 1])
                sums[time, row, x : x + 1, :] = jnp.where(ok, part, 0.0)
        for spot, (side, line) in enumerate(((1, 1), (0, 0), (0, 1), (2, 0))):
            part = jnp.where(row_in[time] & col_in[spot], dots[time, side, line : line + 1, :], 0.0)
            for row in range(3):
                tops[time, row, spot : spot + 1, :] = part

    def gradients(time, row):
        for col in range(2):
            rows, slopes = window(qa, time, col), window(doa, time, col)
            weight = jnp.concatenate([sums[time, row, 3 * col + x : 3 * col + x + 1, :] for x in range(3)], axis=1)
            middle = jnp.concatenate([tops[time, row, col + x : col + x + 1, :] for x in range(3)], axis=1)
            probs = raised[time, row, col].astype(F32) * weight
            grads = (probs * (dot(va[row, col], slopes, NT) - middle)).astype(BF16)
            dv[row, col] += dot(probs.astype(BF16), slopes, NN)
            dk[row, col] += dot(grads, rows, NN)
            part = dot(ka[row, col], grads, TN)
            for x in range(3):
                dq[time, col + x] += part[:, x * tile : (x + 1) * tile]

    returns = []
    for src, dst, step in (
        (send_k.at[0], key_in.at[1], H_DOWN),
        (send_v.at[0], value_in.at[1], H_DOWN),
        (send_k.at[1], key_in.at[0], H_UP),
        (send_v.at[1], value_in.at[0], H_UP),
        (send_q.at[0], time_in.at[1], T_DOWN),
        (send_q.at[1], time_in.at[0], T_UP),
        (edge.at[0], width_in.at[1], W_DOWN),
        (edge.at[1], width_in.at[0], W_UP),
    ):
        returns.append((links.copy(src, dst, number, step), there(step), there(back(step)), dst))
        number += 1

    def give(entries):
        for copy, goes, _, _ in entries:
            pl.when(goes)(copy.start)

    def take(entries):
        for copy, _, comes, dst in entries:

            @pl.when(jnp.logical_not(comes))
            def _():
                dst[...] = jnp.zeros(dst.shape, dst.dtype)

            pl.when(comes)(copy.wait_recv)

    for turn, row in ((0, 0), (1, 2)):
        each(0, 3, lambda x: gradients(x, row))
        send_k[turn] = dk[row].astype(BF16)
        send_v[turn] = dv[row].astype(BF16)
        give(returns[2 * turn : 2 * turn + 2])
    each(0, 2, lambda x: gradients(2 * x, 1))
    for turn, time in ((0, 0), (1, 2)):
        send_q[turn] = dq[time].astype(BF16)
    give(returns[4:6])
    gradients(1, 1)
    take(returns[4:6])
    for turn, spot in ((0, 0), (1, 3)):
        total = dq[1, spot] + time_in[0, spot].astype(F32) + time_in[1, spot].astype(F32)
        edge[turn] = total.astype(BF16)
    give(returns[6:8])
    take(returns[0:4])
    for spot in range(2):
        total = dk[1, spot] + key_in[0, spot].astype(F32) + key_in[1, spot].astype(F32)
        out_dk[spot] = (total * scale).astype(BF16)
        total = dv[1, spot] + value_in[0, spot].astype(F32) + value_in[1, spot].astype(F32)
        out_dv[spot] = total.astype(BF16)
    take(returns[6:8])
    for spot in range(2):
        total = dq[1, 1 + spot] + width_in[spot].astype(F32)
        total = total + time_in[0, 1 + spot].astype(F32) + time_in[1, 1 + spot].astype(F32)
        out_dq[spot] = (total * scale).T.astype(BF16)
    for width, time, height, fans in groups:
        for copy, goes, _ in width + time + height + [fan[:3] for fan in fans]:
            pl.when(goes)(copy.wait_send)
    for copy, goes, _ in small + [x[:3] for x in returns]:
        pl.when(goes)(copy.wait_send)


def shape(*dims, dtype=BF16):
    return jax.ShapeDtypeStruct(dims, dtype)


def on_device(sizes, queries, key_tiles, value_tiles, forward_out, out_grad, pattern, tile_active):
    whole = queries.shape
    tile, feat = whole[4], whole[5]
    scale = 1.0 / math.sqrt(feat)
    q, k, v, fo, do = (
        x.reshape(2, tile, feat) for x in (queries, key_tiles, value_tiles, forward_out, out_grad)
    )
    active = tile_active.reshape(-1, tile_active.shape[2])
    hbm = pl.BlockSpec(memory_space=pltpu.HBM)
    vmem = pl.BlockSpec(memory_space=pltpu.VMEM)
    smem = pl.BlockSpec(memory_space=pltpu.SMEM)
    dma = pltpu.SemaphoreType.DMA

    dq, dk, dv = pl.pallas_call(
        functools.partial(attend_kernel, sizes, scale),
        out_shape=[shape(2, tile, feat)] * 3,
        in_specs=[smem] * 2 + [hbm] * 5,
        out_specs=[vmem] * 3,
        scratch_shapes=[
            pltpu.VMEM((3, 4, tile, feat), BF16),
            pltpu.VMEM((3, 4, tile, feat), BF16),
            pltpu.VMEM((3, 2, tile, feat), BF16),
            pltpu.VMEM((3, 2, tile, feat), BF16),
            pltpu.VMEM((2, tile, feat), BF16),
            pltpu.VMEM((3, 3, 3, 8, tile), F32),
            pltpu.VMEM((3, 3, 8, tile), F32),
            pltpu.VMEM((3, 3, 8, tile), F32),
            pltpu.VMEM((3, 3, 8, tile), F32),
            pltpu.VMEM((3, 3, 2, tile, 3 * tile), BF16),
            pltpu.VMEM((3, 4, feat, tile), F32),
            pltpu.VMEM((3, 2, tile, feat), F32),
            pltpu.VMEM((3, 2, tile, feat), F32),
            pltpu.VMEM((2, 4, feat, tile), BF16),
            pltpu.VMEM((2, 2, tile, feat), BF16),
            pltpu.VMEM((2, 2, tile, feat), BF16),
            pltpu.VMEM((2, 4, feat, tile), BF16),
            pltpu.VMEM((2, 2, tile, feat), BF16),
            pltpu.VMEM((2, 2, tile, feat), BF16),
            pltpu.VMEM((2, feat, tile), BF16),
            pltpu.VMEM((2, feat, tile), BF16),
            dma((5,)),
            dma((60,)),
            dma((60,)),
        ],
        compiler_params=pltpu.CompilerParams(
            collective_id=0, has_side_effects=True, vmem_limit_bytes=60 << 20
        ),
        name="attend",
    )(pattern, active, q, do, k, v, fo)
    return dq.reshape(whole), dk.reshape(whole), dv.reshape(whole)


def solution(mesh):
    tiles = P("ta", "ha", "wa", None, None, None)
    sizes = tuple(mesh.shape[axis] for axis in ("ta", "ha", "wa"))
    return jax.shard_map(
        functools.partial(on_device, sizes),
        mesh=mesh,
        in_specs=(tiles,) * 5 + (P(), P()),
        out_specs=(tiles,) * 3,
        check_vma=False,
    )
```

```python
import functools
import math

import jax
import jax.numpy as jnp
from jax import lax
from jax.experimental import pallas as pl
from jax.experimental.pallas import tpu as pltpu
from jax.sharding import PartitionSpec as P

MESH = pl.DeviceIdType.MESH
F32 = jnp.float32
BF16 = jnp.bfloat16
NT = (((1,), (1,)), ((), ()))
TN = (((0,), (0,)), ((), ()))
NN = (((1,), (0,)), ((), ()))
LOW = -1e30


def dot(left, right, form):
    return lax.dot_general(left, right, form, preferred_element_type=F32)


def position():
    return lax.axis_index("ta"), lax.axis_index("ha"), lax.axis_index("wa")


class Links:
    def __init__(self, sizes, send_sem, recv_sem):
        self.sizes = sizes
        self.at = position()
        self.send_sem = send_sem
        self.recv_sem = recv_sem

    def there(self, step):
        found = None
        for place, size, by in zip(self.at, self.sizes, step):
            if by:
                ok = (place + by >= 0) & (place + by < size)
                found = ok if found is None else found & ok
        return found

    def device(self, step):
        return tuple(
            lax.rem(place + by + size, size) for place, size, by in zip(self.at, self.sizes, step)
        )

    def greet(self, steps):
        barrier = pltpu.get_barrier_semaphore()
        count = 0
        for step in steps:
            count = count + self.there(step).astype(jnp.int32)

            @pl.when(self.there(step))
            def _():
                pl.semaphore_signal(
                    barrier, inc=1, device_id=self.device(step), device_id_type=MESH
                )

        pl.semaphore_wait(barrier, count)

    def copy(self, src, dst, number, step):
        return pltpu.make_async_remote_copy(
            src_ref=src,
            dst_ref=dst,
            send_sem=self.send_sem.at[number],
            recv_sem=self.recv_sem.at[number],
            device_id=self.device(step),
            device_id_type=MESH,
        )


def back(step):
    return tuple(-by for by in step)


W_UP, W_DOWN, T_UP, T_DOWN, H_UP, H_DOWN = (
    (0, 0, 1),
    (0, 0, -1),
    (1, 0, 0),
    (-1, 0, 0),
    (0, 1, 0),
    (0, -1, 0),
)


def all_there(*conditions):
    return functools.reduce(jnp.logical_and, conditions)


PLANE = [(dt, dw) for dt in (-1, 0, 1) for dw in (-1, 0, 1) if (dt, dw) != (0, 0)]
WIDE = [(dt, dw) for dt in (-2, -1, 0, 1, 2) for dw in (-1, 0, 1) if (dt, dw) != (0, 0)]


def side_of(dw):
    return dw % 3


PAIRS = [(col, shift) for col in range(2) for shift in range(3)]


def attend_kernel(
    sizes, scale, pattern, active, q, do, k, v, fo, out_dq, out_dk, out_dv,
    qa, doa, ka, va, own_fo, inbox, dots, tops, sums, raised, dq, dk, dv,
    send_q, send_k, send_v, time_in, key_in, value_in, edge, width_in, local_sem, send_sem, recv_sem,
):
    links = Links(sizes, send_sem, recv_sem)
    there = links.there
    t, h, w = links.at
    nt, nh, nw = sizes
    tile = q.shape[1]
    factor = scale * math.log2(math.e)
    row_in = [t > 0, t >= 0, t < nt - 1]
    col_in = [w > 0, w >= 0, w >= 0, w < nw - 1]

    stay = [
        pltpu.make_async_copy(src, dst, local_sem.at[spot])
        for spot, (src, dst) in enumerate(
            (
                (do, doa.at[1, pl.ds(1, 2)]),
                (fo, own_fo),
                (q, qa.at[1, pl.ds(1, 2)]),
                (k, ka.at[1]),
                (v, va.at[1]),
            )
        )
    ]
    for copy in stay:
        copy.start()
    links.greet([(dt, 0, dw) for dt, dw in WIDE] + [H_UP, H_DOWN])

    groups = []
    number = 0
    for rows, rows_all, cols, cols_all in ((q, qa, k, ka), (do, doa, v, va)):
        width = [
            (links.copy(rows.at[1], rows_all.at[1, 0], number, W_UP), there(W_UP), there(W_DOWN)),
            (links.copy(rows.at[0], rows_all.at[1, 3], number + 1, W_DOWN), there(W_DOWN), there(W_UP)),
        ]
        time = [
            (links.copy(rows, rows_all.at[0, pl.ds(1, 2)], number + 2, T_UP), there(T_UP), there(T_DOWN)),
            (links.copy(rows, rows_all.at[2, pl.ds(1, 2)], number + 3, T_DOWN), there(T_DOWN), there(T_UP)),
        ]
        height = [
            (links.copy(cols, cols_all.at[0], number + 4, H_UP), there(H_UP), there(H_DOWN)),
            (links.copy(cols, cols_all.at[2], number + 5, H_DOWN), there(H_DOWN), there(H_UP)),
        ]
        number += 6
        fans = []
        for spot, has in ((0, there(W_DOWN)), (3, there(W_UP))):
            for step, slot in ((T_UP, 0), (T_DOWN, 2)):
                fan = links.copy(rows_all.at[1, spot], rows_all.at[slot, spot], number, step)
                fans.append((fan, has & there(step), has & there(back(step)), slot))
                number += 1
        groups.append((width, time, height, fans))

    def send(group):
        width, time, height, _ = group
        for copy, goes, _ in width + time + height:
            pl.when(goes)(copy.start)

    def arrive(entries):
        for copy, _, comes in entries:
            pl.when(comes)(copy.wait_recv)

    def forward(group):
        width, _, _, fans = group
        arrive(width)
        for fan, goes, _, _ in fans:
            pl.when(goes)(fan.start)

    send(groups[0])
    stay[0].wait()
    stay[1].wait()
    for spot in range(2):
        both = doa[1, 1 + spot].astype(F32) * own_fo[spot].astype(F32)
        dots[1, 0, spot : spot + 1, :] = jnp.sum(both.T, axis=0, keepdims=True)
    small = []
    for dt, dw in PLANE:
        step = (dt, 0, dw)
        copy = links.copy(dots.at[1, 0], dots.at[1 - dt, side_of(dw)], number, step)
        number += 1
        pl.when(there(step))(copy.start)
        small.append((copy, there(step), there(back(step))))

    def clear(ref, *spot):
        ref[spot] = jnp.zeros(ref.shape[len(spot) :], ref.dtype)

    def clear_sums(x):
        for y in range(4):
            clear(dq, x, y)
        for y in range(2):
            clear(dk, x, y)
            clear(dv, x, y)

    for time in range(3):
        for spot in range(4):
            if (time, spot) not in ((1, 1), (1, 2)):

                @pl.when(jnp.logical_not(row_in[time] & col_in[spot]))
                def _():
                    clear(qa, time, spot)
                    clear(doa, time, spot)

    for row, step in ((0, H_DOWN), (2, H_UP)):

        @pl.when(jnp.logical_not(there(step)))
        def _():
            clear(ka, row)
            clear(va, row)

    def allowed(time, row):
        key_h = h + row - 1
        key_in = (key_h >= 0) & (key_h < nh)
        line = t * nh + jnp.clip(key_h, 0, nh - 1)
        found = []
        for col, shift in PAIRS:
            offset = 9 * (2 - time) + 3 * row + 2 - shift
            on = (active[line, 2 * w + col] == 1) & (pattern[0, offset] == 1)
            inside = key_in & row_in[time] & col_in[col + shift]
            found.append(inside & (on | (offset == 13)))
        return found

    def window(ref, time, col):
        return ref[time, pl.ds(col, 3)].reshape(3 * tile, -1)

    def raise_scores(time, row, spots):
        for col, shift in PAIRS:
            if col + shift in spots:
                x = dot(ka[row, col], qa[time, col + shift], NT) * factor
                high = jnp.max(x, axis=0, keepdims=True)
                x = jnp.exp2(x - high)
                raised[time, row, col, :, shift * tile : (shift + 1) * tile] = x.astype(BF16)
                line = 3 * col + shift
                tops[time, row, line : line + 1, :] = high
                sums[time, row, line : line + 1, :] = jnp.sum(x, axis=0, keepdims=True)

    def publish(time):
        nonlocal number
        terms = [[] for _ in range(4)]
        for row in range(3):
            for x, ((col, shift), ok) in enumerate(zip(PAIRS, allowed(time, row))):
                high = jnp.where(ok, tops[time, row, x : x + 1, :], LOW)
                terms[col + shift].append((high, jnp.where(ok, sums[time, row, x : x + 1, :], 0.0)))
        for spot in range(4):
            top = functools.reduce(jnp.maximum, [x for x, _ in terms[spot]])
            half, line = spot // 2, spot % 2
            inbox[time, time, 0, half, line : line + 1, :] = top
            total = sum(y * jnp.exp2(x - top) for x, y in terms[spot])
            inbox[time, time, 0, half, 2 + line : 3 + line, :] = total
        for dt in (time - 2, time - 1, time):
            for dw in (-1, 0, 1):
                if (dt, dw) == (0, 0):
                    continue
                step = (dt, 0, dw)
                src, slot = inbox.at[time, time, 0], inbox.at[time - dt, time, 0]
                if dw:
                    half = (dw + 1) // 2
                    src, slot = src.at[half], inbox.at[time - dt, time, 1, 1 - half]
                copy = links.copy(src, slot, number, step)
                number += 1
                goes = row_in[time] & there(step)
                pl.when(goes)(copy.start)
                small.append((copy, goes, row_in[time - dt] & there(back(step))))

    def each(first, last, act):
        def step(x, carried):
            act(x)
            return carried

        lax.fori_loop(first, last, step, 0)

    own, outer = (1, 2), (0, 3)
    stay[2].wait()
    stay[3].wait()
    raise_scores(1, 1, own)
    forward(groups[0])
    arrive(groups[0][2])
    send(groups[1])
    each(0, 2, lambda x: raise_scores(1, 2 * x, own))
    each(0, 3, lambda x: raise_scores(1, x, outer))
    publish(1)
    forward(groups[1])
    arrive(groups[0][1])
    each(0, 6, lambda x: raise_scores(2 * (x // 3), x % 3, own))
    for time in (0, 2):
        arrive([fan[:3] for fan in groups[0][3] if fan[3] == time])
        each(0, 3, lambda x: raise_scores(time, x, outer))
        publish(time)
    each(0, 3, clear_sums)
    arrive(groups[1][1] + groups[1][2] + [fan[:3] for fan in groups[1][3]])
    stay[4].wait()
    arrive(small)

    for time in range(3):
        log_total = []
        for half, beside in ((0, w > 0), (1, w < nw - 1)):
            terms = []
            for sender in range(3):
                ok = (t + time - sender >= 0) & (t + time - sender < nt)
                for side, good in ((0, ok), (1, ok & beside)):
                    both = inbox[time, sender, side, half]
                    terms.append((jnp.where(good, both[0:2], LOW), jnp.where(good, both[2:4], 0.0)))
            top = functools.reduce(jnp.maximum, [x for x, _ in terms])
            log_total.append(top + jnp.log2(sum(y * jnp.exp2(x - top) for x, y in terms)))
        log_total = jnp.concatenate(log_total, axis=0)
        for row in range(3):
            for x, ((col, shift), ok) in enumerate(zip(PAIRS, allowed(time, row))):
                part = jnp.exp2(tops[time, row, x : x + 1, :] - log_total[col + shift : col + shift + 1])
                sums[time, row, x : x + 1, :] = jnp.where(ok, part, 0.0)
        for spot, (side, line) in enumerate(((1, 1), (0, 0), (0, 1), (2, 0))):
            part = jnp.where(row_in[time] & col_in[spot], dots[time, side, line : line + 1, :], 0.0)
            for row in range(3):
                tops[time, row, spot : spot + 1, :] = part

    def gradients(time, row, cols=(0, 1)):
        for col in cols:
            rows, slopes = window(qa, time, col), window(doa, time, col)
            weight = jnp.concatenate([sums[time, row, 3 * col + x : 3 * col + x + 1, :] for x in range(3)], axis=1)
            middle = jnp.concatenate([tops[time, row, col + x : col + x + 1, :] for x in range(3)], axis=1)
            probs = raised[time, row, col].astype(F32) * weight
            grads = (probs * (dot(va[row, col], slopes, NT) - middle)).astype(BF16)
            dv[row, col] += dot(probs.astype(BF16), slopes, NN)
            dk[row, col] += dot(grads, rows, NN)
            part = dot(ka[row, col], grads, TN)
            for x in range(3):
                dq[time, col + x] += part[:, x * tile : (x + 1) * tile]

    returns = []
    for src, dst, step in (
        (send_k.at[0], key_in.at[1], H_DOWN),
        (send_v.at[0], value_in.at[1], H_DOWN),
        (send_k.at[1, 0], key_in.at[0, 0], H_UP),
        (send_v.at[1, 0], value_in.at[0, 0], H_UP),
        (send_k.at[1, 1], key_in.at[0, 1], H_UP),
        (send_v.at[1, 1], value_in.at[0, 1], H_UP),
        (send_q.at[0], time_in.at[1], T_DOWN),
        (send_q.at[1], time_in.at[0], T_UP),
        (edge.at[0], width_in.at[1], W_DOWN),
        (edge.at[1], width_in.at[0], W_UP),
    ):
        returns.append((links.copy(src, dst, number, step), there(step), there(back(step)), dst))
        number += 1

    def give(entries):
        for copy, goes, _, _ in entries:
            pl.when(goes)(copy.start)

    def take(entries):
        for copy, _, comes, dst in entries:

            @pl.when(jnp.logical_not(comes))
            def _():
                dst[...] = jnp.zeros(dst.shape, dst.dtype)

            pl.when(comes)(copy.wait_recv)

    each(0, 3, lambda x: gradients(2 * x % 3, 0))
    send_k[0] = dk[0].astype(BF16)
    send_v[0] = dv[0].astype(BF16)
    give(returns[0:2])

    def outer_rows(x):
        gradients(2 * (x // 2), 2 - x % 2)
        for turn in range(2):

            @pl.when(x == 2 * turn + 1)
            def _():
                send_q[turn] = dq[2 * turn].astype(BF16)
                give(returns[6 + turn : 7 + turn])

    each(0, 4, outer_rows)
    for col in range(2):
        gradients(1, 2, (col,))
        send_k[1, col] = dk[2, col].astype(BF16)
        send_v[1, col] = dv[2, col].astype(BF16)
        give(returns[2 + 2 * col : 4 + 2 * col])
    gradients(1, 1)
    take(returns[6:8])
    for turn, spot in ((0, 0), (1, 3)):
        total = dq[1, spot] + time_in[0, spot].astype(F32) + time_in[1, spot].astype(F32)
        edge[turn] = total.astype(BF16)
    give(returns[8:10])
    take(returns[0:6])
    for spot in range(2):
        total = dk[1, spot] + key_in[0, spot].astype(F32) + key_in[1, spot].astype(F32)
        out_dk[spot] = (total * scale).astype(BF16)
        total = dv[1, spot] + value_in[0, spot].astype(F32) + value_in[1, spot].astype(F32)
        out_dv[spot] = total.astype(BF16)
    take(returns[8:10])
    for spot in range(2):
        total = dq[1, 1 + spot] + width_in[spot].astype(F32)
        total = total + time_in[0, 1 + spot].astype(F32) + time_in[1, 1 + spot].astype(F32)
        out_dq[spot] = (total * scale).T.astype(BF16)
    for width, time, height, fans in groups:
        for copy, goes, _ in width + time + height + [fan[:3] for fan in fans]:
            pl.when(goes)(copy.wait_send)
    for copy, goes, _ in small + [x[:3] for x in returns]:
        pl.when(goes)(copy.wait_send)


def settle_kernel(*refs):
    ins, outs, held, sems = refs[:3], refs[3:6], refs[6:9], refs[9]
    first = [pltpu.make_async_copy(src, dst, sems.at[x]) for x, (src, dst) in enumerate(zip(ins, held))]
    then = [pltpu.make_async_copy(src, dst, sems.at[3 + x]) for x, (src, dst) in enumerate(zip(held, outs))]
    for copy in first:
        copy.start()
    for one, two in zip(first, then):
        one.wait()
        two.start()
    for copy in then:
        copy.wait()


def shape(*dims, dtype=BF16):
    return jax.ShapeDtypeStruct(dims, dtype)


def on_device(sizes, queries, key_tiles, value_tiles, forward_out, out_grad, pattern, tile_active):
    whole = queries.shape
    tile, feat = whole[4], whole[5]
    scale = 1.0 / math.sqrt(feat)
    q, k, v, fo, do = (
        x.reshape(2, tile, feat) for x in (queries, key_tiles, value_tiles, forward_out, out_grad)
    )
    active = tile_active.reshape(-1, tile_active.shape[2])
    hbm = pl.BlockSpec(memory_space=pltpu.HBM)
    vmem = pl.BlockSpec(memory_space=pltpu.VMEM)
    smem = pl.BlockSpec(memory_space=pltpu.SMEM)
    dma = pltpu.SemaphoreType.DMA

    dq, dk, dv = pl.pallas_call(
        functools.partial(attend_kernel, sizes, scale),
        out_shape=[shape(2, tile, feat)] * 3,
        in_specs=[smem] * 2 + [hbm] * 5,
        out_specs=[vmem] * 3,
        scratch_shapes=[
            pltpu.VMEM((3, 4, tile, feat), BF16),
            pltpu.VMEM((3, 4, tile, feat), BF16),
            pltpu.VMEM((3, 2, tile, feat), BF16),
            pltpu.VMEM((3, 2, tile, feat), BF16),
            pltpu.VMEM((2, tile, feat), BF16),
            pltpu.VMEM((3, 3, 2, 2, 4, tile), F32),
            pltpu.VMEM((3, 3, 2, tile), F32),
            pltpu.VMEM((3, 3, 8, tile), F32),
            pltpu.VMEM((3, 3, 8, tile), F32),
            pltpu.VMEM((3, 3, 2, tile, 3 * tile), BF16),
            pltpu.VMEM((3, 4, feat, tile), F32),
            pltpu.VMEM((3, 2, tile, feat), F32),
            pltpu.VMEM((3, 2, tile, feat), F32),
            pltpu.VMEM((2, 4, feat, tile), BF16),
            pltpu.VMEM((2, 2, tile, feat), BF16),
            pltpu.VMEM((2, 2, tile, feat), BF16),
            pltpu.VMEM((2, 4, feat, tile), BF16),
            pltpu.VMEM((2, 2, tile, feat), BF16),
            pltpu.VMEM((2, 2, tile, feat), BF16),
            pltpu.VMEM((2, feat, tile), BF16),
            pltpu.VMEM((2, feat, tile), BF16),
            dma((5,)),
            dma((62,)),
            dma((62,)),
        ],
        compiler_params=pltpu.CompilerParams(
            collective_id=0, has_side_effects=True, vmem_limit_bytes=60 << 20
        ),
        name="attend",
    )(pattern, active, q, do, k, v, fo)
    dq, dk, dv = pl.pallas_call(
        settle_kernel,
        out_shape=[shape(2, tile, feat)] * 3,
        in_specs=[hbm] * 3,
        out_specs=[hbm] * 3,
        scratch_shapes=[pltpu.VMEM((2, tile, feat), BF16)] * 3 + [dma((6,))],
        compiler_params=pltpu.CompilerParams(vmem_limit_bytes=60 << 20),
        name="settle",
    )(dq, dk, dv)
    return dq.reshape(whole), dk.reshape(whole), dv.reshape(whole)


def solution(mesh):
    tiles = P("ta", "ha", "wa", None, None, None)
    sizes = tuple(mesh.shape[axis] for axis in ("ta", "ha", "wa"))
    return jax.shard_map(
        functools.partial(on_device, sizes),
        mesh=mesh,
        in_specs=(tiles,) * 5 + (P(), P()),
        out_specs=(tiles,) * 3,
        check_vma=False,
    )
```

```python
import functools
import math

import jax
import jax.numpy as jnp
from jax import lax
from jax.experimental import pallas as pl
from jax.experimental.pallas import tpu as pltpu
from jax.sharding import PartitionSpec as P

MESH = pl.DeviceIdType.MESH
F32 = jnp.float32
BF16 = jnp.bfloat16
NT = (((1,), (1,)), ((), ()))
TN = (((0,), (0,)), ((), ()))
NN = (((1,), (0,)), ((), ()))
LOW = -1e30


def dot(left, right, form):
    return lax.dot_general(left, right, form, preferred_element_type=F32)


def position():
    return lax.axis_index("ta"), lax.axis_index("ha"), lax.axis_index("wa")


class Links:
    def __init__(self, sizes, send_sem, recv_sem):
        self.sizes = sizes
        self.at = position()
        self.send_sem = send_sem
        self.recv_sem = recv_sem

    def there(self, step):
        found = None
        for place, size, by in zip(self.at, self.sizes, step):
            if by:
                ok = (place + by >= 0) & (place + by < size)
                found = ok if found is None else found & ok
        return found

    def device(self, step):
        return tuple(
            lax.rem(place + by + size, size) for place, size, by in zip(self.at, self.sizes, step)
        )

    def greet(self, steps):
        barrier = pltpu.get_barrier_semaphore()
        count = 0
        for step in steps:
            count = count + self.there(step).astype(jnp.int32)

            @pl.when(self.there(step))
            def _():
                pl.semaphore_signal(
                    barrier, inc=1, device_id=self.device(step), device_id_type=MESH
                )

        pl.semaphore_wait(barrier, count)

    def copy(self, src, dst, number, step):
        return pltpu.make_async_remote_copy(
            src_ref=src,
            dst_ref=dst,
            send_sem=self.send_sem.at[number],
            recv_sem=self.recv_sem.at[number],
            device_id=self.device(step),
            device_id_type=MESH,
        )


def back(step):
    return tuple(-by for by in step)


W_UP, W_DOWN, T_UP, T_DOWN, H_UP, H_DOWN = (
    (0, 0, 1),
    (0, 0, -1),
    (1, 0, 0),
    (-1, 0, 0),
    (0, 1, 0),
    (0, -1, 0),
)


def all_there(*conditions):
    return functools.reduce(jnp.logical_and, conditions)


PLANE = [(dt, dw) for dt in (-1, 0, 1) for dw in (-1, 0, 1) if (dt, dw) != (0, 0)]
WIDE = [(dt, dw) for dt in (-2, -1, 0, 1, 2) for dw in (-1, 0, 1) if (dt, dw) != (0, 0)]


def side_of(dw):
    return dw % 3


PAIRS = [(col, shift) for col in range(2) for shift in range(3)]


def attend_kernel(
    sizes, scale, pattern, active, q, do, k, v, fo, out_dq, out_dk, out_dv,
    qa, doa, ka, va, own_fo, inbox, dots, tops, sums, raised, dq, dk, dv,
    send_q, send_k, send_v, time_in, corner_in, key_in, value_in, edge, width_in, local_sem, send_sem, recv_sem,
):
    links = Links(sizes, send_sem, recv_sem)
    there = links.there
    t, h, w = links.at
    nt, nh, nw = sizes
    tile = q.shape[1]
    factor = scale * math.log2(math.e)
    row_in = [t > 0, t >= 0, t < nt - 1]
    col_in = [w > 0, w >= 0, w >= 0, w < nw - 1]

    stay = [
        pltpu.make_async_copy(src, dst, local_sem.at[spot])
        for spot, (src, dst) in enumerate(
            (
                (do, doa.at[1, pl.ds(1, 2)]),
                (fo, own_fo),
                (q, qa.at[1, pl.ds(1, 2)]),
                (k, ka.at[1]),
                (v, va.at[1]),
            )
        )
    ]
    for copy in stay:
        copy.start()
    links.greet([(dt, 0, dw) for dt, dw in WIDE] + [H_UP, H_DOWN])

    groups = []
    number = 0
    for rows, rows_all, cols, cols_all in ((q, qa, k, ka), (do, doa, v, va)):
        width = [
            (links.copy(rows.at[1], rows_all.at[1, 0], number, W_UP), there(W_UP), there(W_DOWN)),
            (links.copy(rows.at[0], rows_all.at[1, 3], number + 1, W_DOWN), there(W_DOWN), there(W_UP)),
        ]
        time = [
            (links.copy(rows, rows_all.at[0, pl.ds(1, 2)], number + 2, T_UP), there(T_UP), there(T_DOWN)),
            (links.copy(rows, rows_all.at[2, pl.ds(1, 2)], number + 3, T_DOWN), there(T_DOWN), there(T_UP)),
        ]
        height = [
            (links.copy(cols, cols_all.at[0], number + 4, H_UP), there(H_UP), there(H_DOWN)),
            (links.copy(cols, cols_all.at[2], number + 5, H_DOWN), there(H_DOWN), there(H_UP)),
        ]
        number += 6
        fans = []
        for spot, has in ((0, there(W_DOWN)), (3, there(W_UP))):
            for step, slot in ((T_UP, 0), (T_DOWN, 2)):
                fan = links.copy(rows_all.at[1, spot], rows_all.at[slot, spot], number, step)
                fans.append((fan, has & there(step), has & there(back(step)), slot))
                number += 1
        groups.append((width, time, height, fans))

    def send(entries):
        for copy, goes, _ in entries:
            pl.when(goes)(copy.start)

    def arrive(entries):
        for copy, _, comes in entries:
            pl.when(comes)(copy.wait_recv)

    def forward(group):
        width, _, _, fans = group
        arrive(width)
        for fan, goes, _, _ in fans:
            pl.when(goes)(fan.start)

    send(groups[0][0] + groups[0][1] + groups[0][2] + groups[1][0])
    stay[0].wait()
    stay[1].wait()
    for spot in range(2):
        both = doa[1, 1 + spot].astype(F32) * own_fo[spot].astype(F32)
        dots[1, 0, spot : spot + 1, :] = jnp.sum(both.T, axis=0, keepdims=True)
    small = []
    for dt, dw in PLANE:
        step = (dt, 0, dw)
        copy = links.copy(dots.at[1, 0], dots.at[1 - dt, side_of(dw)], number, step)
        number += 1
        pl.when(there(step))(copy.start)
        small.append((copy, there(step), there(back(step))))

    def clear(ref, *spot):
        ref[spot] = jnp.zeros(ref.shape[len(spot) :], ref.dtype)

    def clear_sums(x):
        for y in range(4):
            clear(dq, x, y)
        for y in range(2):
            clear(dk, x, y)
            clear(dv, x, y)

    for time in range(3):
        for spot in range(4):
            if (time, spot) not in ((1, 1), (1, 2)):

                @pl.when(jnp.logical_not(row_in[time] & col_in[spot]))
                def _():
                    clear(qa, time, spot)
                    clear(doa, time, spot)

    for row, step in ((0, H_DOWN), (2, H_UP)):

        @pl.when(jnp.logical_not(there(step)))
        def _():
            clear(ka, row)
            clear(va, row)

    def allowed(time, row):
        key_h = h + row - 1
        key_in = (key_h >= 0) & (key_h < nh)
        line = t * nh + jnp.clip(key_h, 0, nh - 1)
        found = []
        for col, shift in PAIRS:
            offset = 9 * (2 - time) + 3 * row + 2 - shift
            on = (active[line, 2 * w + col] == 1) & (pattern[0, offset] == 1)
            inside = key_in & row_in[time] & col_in[col + shift]
            found.append(inside & (on | (offset == 13)))
        return found

    def raise_scores(time, rows, spots):
        taken = [(row, col, shift) for row in rows for col, shift in PAIRS if col + shift in spots]
        scores = [dot(ka[row, col], qa[time, col + shift], NT) * factor for row, col, shift in taken]
        highs = [jnp.max(x, axis=0, keepdims=True) for x in scores]
        for (row, col, shift), x, high in zip(taken, scores, highs):
            x = jnp.exp2(x - high)
            raised[time, row, col, :, shift * tile : (shift + 1) * tile] = x.astype(BF16)
            line = 3 * col + shift
            tops[time, row, line : line + 1, :] = high
            sums[time, row, line : line + 1, :] = jnp.sum(x, axis=0, keepdims=True)

    def publish(time):
        nonlocal number
        terms = [[] for _ in range(4)]
        for row in range(3):
            for x, ((col, shift), ok) in enumerate(zip(PAIRS, allowed(time, row))):
                high = jnp.where(ok, tops[time, row, x : x + 1, :], LOW)
                terms[col + shift].append((high, jnp.where(ok, sums[time, row, x : x + 1, :], 0.0)))
        for spot in range(4):
            top = functools.reduce(jnp.maximum, [x for x, _ in terms[spot]])
            half, line = spot // 2, spot % 2
            inbox[time, time, 0, half, line : line + 1, :] = top
            total = sum(y * jnp.exp2(x - top) for x, y in terms[spot])
            inbox[time, time, 0, half, 2 + line : 3 + line, :] = total
        for dt in (time - 2, time - 1, time):
            for dw in (-1, 0, 1):
                if (dt, dw) == (0, 0):
                    continue
                step = (dt, 0, dw)
                src, slot = inbox.at[time, time, 0], inbox.at[time - dt, time, 0]
                if dw:
                    half = (dw + 1) // 2
                    src, slot = src.at[half], inbox.at[time - dt, time, 1, 1 - half]
                copy = links.copy(src, slot, number, step)
                number += 1
                goes = row_in[time] & there(step)
                pl.when(goes)(copy.start)
                small.append((copy, goes, row_in[time - dt] & there(back(step))))

    def each(first, last, act):
        def step(x, carried):
            act(x)
            return carried

        lax.fori_loop(first, last, step, 0)

    own, outer = (1, 2), (0, 3)
    stay[2].wait()
    stay[3].wait()
    raise_scores(1, (1,), own)
    forward(groups[0])
    arrive(groups[0][2])
    send(groups[1][1] + groups[1][2])
    raise_scores(1, (0, 2), own)
    raise_scores(1, (0, 1, 2), outer)
    publish(1)
    forward(groups[1])
    arrive(groups[0][1])
    each(0, 2, lambda x: raise_scores(2 * x, (0, 1, 2), own))
    for time in (0, 2):
        arrive([fan[:3] for fan in groups[0][3] if fan[3] == time])
        raise_scores(time, (0, 1, 2), outer)
        publish(time)
    each(0, 3, clear_sums)
    arrive(groups[1][1] + groups[1][2] + [fan[:3] for fan in groups[1][3]])
    stay[4].wait()
    arrive(small)

    for time in range(3):
        log_total = []
        for half, beside in ((0, w > 0), (1, w < nw - 1)):
            terms = []
            for sender in range(3):
                ok = (t + time - sender >= 0) & (t + time - sender < nt)
                for side, good in ((0, ok), (1, ok & beside)):
                    both = inbox[time, sender, side, half]
                    terms.append((jnp.where(good, both[0:2], LOW), jnp.where(good, both[2:4], 0.0)))
            top = functools.reduce(jnp.maximum, [x for x, _ in terms])
            log_total.append(top + jnp.log2(sum(y * jnp.exp2(x - top) for x, y in terms)))
        log_total = jnp.concatenate(log_total, axis=0)
        for row in range(3):
            for x, ((col, shift), ok) in enumerate(zip(PAIRS, allowed(time, row))):
                part = jnp.exp2(tops[time, row, x : x + 1, :] - log_total[col + shift : col + shift + 1])
                sums[time, row, x : x + 1, :] = jnp.where(ok, part, 0.0)
        for spot, (side, line) in enumerate(((1, 1), (0, 0), (0, 1), (2, 0))):
            part = jnp.where(row_in[time] & col_in[spot], dots[time, side, line : line + 1, :], 0.0)
            for row in range(3):
                tops[time, row, spot : spot + 1, :] = part

    def gradients(time, row, parts=((0, 0, 3), (1, 0, 3))):
        for col, first, many in parts:
            begin, shifts = col + first, range(first, first + many)
            rows = qa[time, begin : begin + many].reshape(many * tile, -1)
            slopes = doa[time, begin : begin + many].reshape(many * tile, -1)
            weight = jnp.concatenate([sums[time, row, 3 * col + x : 3 * col + x + 1, :] for x in shifts], axis=1)
            middle = jnp.concatenate([tops[time, row, col + x : col + x + 1, :] for x in shifts], axis=1)
            probs = raised[time, row, col, :, first * tile : (first + many) * tile].astype(F32) * weight
            grads = (probs * (dot(va[row, col], slopes, NT) - middle)).astype(BF16)
            dv[row, col] += dot(probs.astype(BF16), slopes, NN)
            dk[row, col] += dot(grads, rows, NN)
            part = dot(ka[row, col], grads, TN)
            for x in range(many):
                dq[time, begin + x] += part[:, x * tile : (x + 1) * tile]

    returns = []
    for src, dst, step in (
        (send_k.at[0], key_in.at[1], H_DOWN),
        (send_v.at[0], value_in.at[1], H_DOWN),
        (send_k.at[1, 0], key_in.at[0, 0], H_UP),
        (send_v.at[1, 0], value_in.at[0, 0], H_UP),
        (send_k.at[1, 1], key_in.at[0, 1], H_UP),
        (send_v.at[1, 1], value_in.at[0, 1], H_UP),
        (send_q.at[0, pl.ds(1, 2)], time_in.at[1], T_DOWN),
        (send_q.at[0, 0], corner_in.at[1, 1], (-1, 0, -1)),
        (send_q.at[0, 3], corner_in.at[1, 0], (-1, 0, 1)),
        (send_q.at[1, pl.ds(1, 2)], time_in.at[0], T_UP),
        (send_q.at[1, 0], corner_in.at[0, 1], (1, 0, -1)),
        (send_q.at[1, 3], corner_in.at[0, 0], (1, 0, 1)),
        (edge.at[0], width_in.at[1], W_DOWN),
        (edge.at[1], width_in.at[0], W_UP),
    ):
        returns.append((links.copy(src, dst, number, step), there(step), there(back(step)), dst))
        number += 1

    def give(entries):
        for copy, goes, _, _ in entries:
            pl.when(goes)(copy.start)

    def take(entries):
        for copy, _, comes, dst in entries:

            @pl.when(jnp.logical_not(comes))
            def _():
                dst[...] = jnp.zeros(dst.shape, dst.dtype)

            pl.when(comes)(copy.wait_recv)

    each(0, 3, lambda x: gradients(2 * x % 3, 0))
    send_k[0] = dk[0].astype(BF16)
    send_v[0] = dv[0].astype(BF16)
    give(returns[0:2])

    def hand_over(turn):
        send_q[turn] = dq[2 * turn].astype(BF16)
        give(returns[6 + 3 * turn : 9 + 3 * turn])

    each(0, 2, lambda x: gradients(0, 2 - x))
    hand_over(0)
    gradients(2, 2)
    for col in range(2):
        gradients(1, 2, ((col, 0, 3),))
        send_k[1, col] = dk[2, col].astype(BF16)
        send_v[1, col] = dv[2, col].astype(BF16)
        give(returns[2 + 2 * col : 4 + 2 * col])
    gradients(2, 1)
    hand_over(1)
    gradients(1, 1, ((0, 0, 1), (1, 2, 1)))
    for turn, spot in ((0, 0), (1, 3)):
        edge[turn] = dq[1, spot].astype(BF16)
    give(returns[12:14])
    gradients(1, 1, ((0, 1, 2), (1, 0, 2)))
    take(returns[0:6])
    for spot in range(2):
        total = dk[1, spot] + key_in[0, spot].astype(F32) + key_in[1, spot].astype(F32)
        out_dk[spot] = (total * scale).astype(BF16)
        total = dv[1, spot] + value_in[0, spot].astype(F32) + value_in[1, spot].astype(F32)
        out_dv[spot] = total.astype(BF16)
    take(returns[6:14])
    for spot in range(2):
        total = dq[1, 1 + spot] + width_in[spot].astype(F32)
        for turn in range(2):
            total = total + time_in[turn, spot].astype(F32) + corner_in[turn, spot].astype(F32)
        out_dq[spot] = (total * scale).T.astype(BF16)
    for width, time, height, fans in groups:
        for copy, goes, _ in width + time + height + [fan[:3] for fan in fans]:
            pl.when(goes)(copy.wait_send)
    for copy, goes, _ in small + [x[:3] for x in returns]:
        pl.when(goes)(copy.wait_send)


def settle_kernel(*refs):
    ins, outs, held, sems = refs[:3], refs[3:6], refs[6:9], refs[9]
    first = [pltpu.make_async_copy(src, dst, sems.at[x]) for x, (src, dst) in enumerate(zip(ins, held))]
    then = [pltpu.make_async_copy(src, dst, sems.at[3 + x]) for x, (src, dst) in enumerate(zip(held, outs))]
    for copy in first:
        copy.start()
    for one, two in zip(first, then):
        one.wait()
        two.start()
    for copy in then:
        copy.wait()


def shape(*dims, dtype=BF16):
    return jax.ShapeDtypeStruct(dims, dtype)


def on_device(sizes, queries, key_tiles, value_tiles, forward_out, out_grad, pattern, tile_active):
    whole = queries.shape
    tile, feat = whole[4], whole[5]
    scale = 1.0 / math.sqrt(feat)
    q, k, v, fo, do = (
        x.reshape(2, tile, feat) for x in (queries, key_tiles, value_tiles, forward_out, out_grad)
    )
    active = tile_active.reshape(-1, tile_active.shape[2])
    hbm = pl.BlockSpec(memory_space=pltpu.HBM)
    vmem = pl.BlockSpec(memory_space=pltpu.VMEM)
    smem = pl.BlockSpec(memory_space=pltpu.SMEM)
    dma = pltpu.SemaphoreType.DMA

    dq, dk, dv = pl.pallas_call(
        functools.partial(attend_kernel, sizes, scale),
        out_shape=[shape(2, tile, feat)] * 3,
        in_specs=[smem] * 2 + [hbm] * 5,
        out_specs=[vmem] * 3,
        scratch_shapes=[
            pltpu.VMEM((3, 4, tile, feat), BF16),
            pltpu.VMEM((3, 4, tile, feat), BF16),
            pltpu.VMEM((3, 2, tile, feat), BF16),
            pltpu.VMEM((3, 2, tile, feat), BF16),
            pltpu.VMEM((2, tile, feat), BF16),
            pltpu.VMEM((3, 3, 2, 2, 4, tile), F32),
            pltpu.VMEM((3, 3, 2, tile), F32),
            pltpu.VMEM((3, 3, 8, tile), F32),
            pltpu.VMEM((3, 3, 8, tile), F32),
            pltpu.VMEM((3, 3, 2, tile, 3 * tile), BF16),
            pltpu.VMEM((3, 4, feat, tile), F32),
            pltpu.VMEM((3, 2, tile, feat), F32),
            pltpu.VMEM((3, 2, tile, feat), F32),
            pltpu.VMEM((2, 4, feat, tile), BF16),
            pltpu.VMEM((2, 2, tile, feat), BF16),
            pltpu.VMEM((2, 2, tile, feat), BF16),
            pltpu.VMEM((2, 2, feat, tile), BF16),
            pltpu.VMEM((2, 2, feat, tile), BF16),
            pltpu.VMEM((2, 2, tile, feat), BF16),
            pltpu.VMEM((2, 2, tile, feat), BF16),
            pltpu.VMEM((2, feat, tile), BF16),
            pltpu.VMEM((2, feat, tile), BF16),
            dma((5,)),
            dma((66,)),
            dma((66,)),
        ],
        compiler_params=pltpu.CompilerParams(
            collective_id=0, has_side_effects=True, vmem_limit_bytes=60 << 20
        ),
        name="attend",
    )(pattern, active, q, do, k, v, fo)
    dq, dk, dv = pl.pallas_call(
        settle_kernel,
        out_shape=[shape(2, tile, feat)] * 3,
        in_specs=[hbm] * 3,
        out_specs=[hbm] * 3,
        scratch_shapes=[pltpu.VMEM((2, tile, feat), BF16)] * 3 + [dma((6,))],
        compiler_params=pltpu.CompilerParams(vmem_limit_bytes=60 << 20),
        name="settle",
    )(dq, dk, dv)
    return dq.reshape(whole), dk.reshape(whole), dv.reshape(whole)


def solution(mesh):
    tiles = P("ta", "ha", "wa", None, None, None)
    sizes = tuple(mesh.shape[axis] for axis in ("ta", "ha", "wa"))
    return jax.shard_map(
        functools.partial(on_device, sizes),
        mesh=mesh,
        in_specs=(tiles,) * 5 + (P(), P()),
        out_specs=(tiles,) * 3,
        check_vma=False,
    )
```

```python
import functools
import math

import jax
import jax.numpy as jnp
from jax import lax
from jax.experimental import pallas as pl
from jax.experimental.pallas import tpu as pltpu
from jax.sharding import PartitionSpec as P

MESH = pl.DeviceIdType.MESH
F32 = jnp.float32
BF16 = jnp.bfloat16
NT = (((1,), (1,)), ((), ()))
TN = (((0,), (0,)), ((), ()))
NN = (((1,), (0,)), ((), ()))
LOW = -1e30


def dot(left, right, form):
    return lax.dot_general(left, right, form, preferred_element_type=F32)


def position():
    return lax.axis_index("ta"), lax.axis_index("ha"), lax.axis_index("wa")


class Links:
    def __init__(self, sizes, send_sem, recv_sem):
        self.sizes = sizes
        self.at = position()
        self.send_sem = send_sem
        self.recv_sem = recv_sem

    def there(self, step):
        found = None
        for place, size, by in zip(self.at, self.sizes, step):
            if by:
                ok = (place + by >= 0) & (place + by < size)
                found = ok if found is None else found & ok
        return found

    def device(self, step):
        return tuple(
            lax.rem(place + by + size, size) for place, size, by in zip(self.at, self.sizes, step)
        )

    def greet(self, steps):
        barrier = pltpu.get_barrier_semaphore()
        count = 0
        for step in steps:
            count = count + self.there(step).astype(jnp.int32)

            @pl.when(self.there(step))
            def _():
                pl.semaphore_signal(
                    barrier, inc=1, device_id=self.device(step), device_id_type=MESH
                )

        pl.semaphore_wait(barrier, count)

    def copy(self, src, dst, number, step):
        return pltpu.make_async_remote_copy(
            src_ref=src,
            dst_ref=dst,
            send_sem=self.send_sem.at[number],
            recv_sem=self.recv_sem.at[number],
            device_id=self.device(step),
            device_id_type=MESH,
        )


def back(step):
    return tuple(-by for by in step)


W_UP, W_DOWN, T_UP, T_DOWN, H_UP, H_DOWN = (
    (0, 0, 1),
    (0, 0, -1),
    (1, 0, 0),
    (-1, 0, 0),
    (0, 1, 0),
    (0, -1, 0),
)


def all_there(*conditions):
    return functools.reduce(jnp.logical_and, conditions)


PLANE = [(dt, dw) for dt in (-1, 0, 1) for dw in (-1, 0, 1) if (dt, dw) != (0, 0)]
WIDE = [(dt, dw) for dt in (-2, -1, 0, 1, 2) for dw in (-1, 0, 1) if (dt, dw) != (0, 0)]


def side_of(dw):
    return dw % 3


PAIRS = [(col, shift) for col in range(2) for shift in range(3)]


def attend_kernel(
    sizes, scale, pattern, active, q, do, k, v, fo, out_dq, out_dk, out_dv,
    qa, doa, ka, va, own_fo, inbox, dots, tops, sums, raised, dq, dk, dv,
    send_q, send_k, send_v, time_in, corner_in, key_in, value_in, edge, width_in, local_sem, send_sem, recv_sem,
):
    links = Links(sizes, send_sem, recv_sem)
    there = links.there
    t, h, w = links.at
    nt, nh, nw = sizes
    tile = q.shape[1]
    factor = scale * math.log2(math.e)
    row_in = [t > 0, t >= 0, t < nt - 1]
    col_in = [w > 0, w >= 0, w >= 0, w < nw - 1]

    stay = [
        pltpu.make_async_copy(src, dst, local_sem.at[spot])
        for spot, (src, dst) in enumerate(
            (
                (do, doa.at[1, pl.ds(1, 2)]),
                (fo, own_fo),
                (q, qa.at[1, pl.ds(1, 2)]),
                (k, ka.at[1]),
                (v, va.at[1]),
            )
        )
    ]
    for copy in stay:
        copy.start()
    links.greet([(dt, 0, dw) for dt, dw in WIDE] + [H_UP, H_DOWN])

    groups = []
    number = 0
    for rows, rows_all, cols, cols_all in ((q, qa, k, ka), (do, doa, v, va)):
        width = [
            (links.copy(rows.at[1], rows_all.at[1, 0], number, W_UP), there(W_UP), there(W_DOWN)),
            (links.copy(rows.at[0], rows_all.at[1, 3], number + 1, W_DOWN), there(W_DOWN), there(W_UP)),
        ]
        time = [
            (links.copy(rows, rows_all.at[0, pl.ds(1, 2)], number + 2, T_UP), there(T_UP), there(T_DOWN)),
            (links.copy(rows, rows_all.at[2, pl.ds(1, 2)], number + 3, T_DOWN), there(T_DOWN), there(T_UP)),
        ]
        height = [
            (links.copy(cols, cols_all.at[0], number + 4, H_UP), there(H_UP), there(H_DOWN)),
            (links.copy(cols, cols_all.at[2], number + 5, H_DOWN), there(H_DOWN), there(H_UP)),
        ]
        number += 6
        fans = []
        for spot, has in ((0, there(W_DOWN)), (3, there(W_UP))):
            for step, slot in ((T_UP, 0), (T_DOWN, 2)):
                fan = links.copy(rows_all.at[1, spot], rows_all.at[slot, spot], number, step)
                fans.append((fan, has & there(step), has & there(back(step)), slot))
                number += 1
        groups.append((width, time, height, fans))

    def send(entries):
        for copy, goes, _ in entries:
            pl.when(goes)(copy.start)

    def arrive(entries):
        for copy, _, comes in entries:
            pl.when(comes)(copy.wait_recv)

    def forward(group):
        width, _, _, fans = group
        arrive(width)
        for fan, goes, _, _ in fans:
            pl.when(goes)(fan.start)

    send(groups[0][0] + groups[0][1] + groups[0][2] + groups[1][0])
    stay[0].wait()
    stay[1].wait()
    for spot in range(2):
        both = doa[1, 1 + spot].astype(F32) * own_fo[spot].astype(F32)
        dots[1, 0, spot : spot + 1, :] = jnp.sum(both.T, axis=0, keepdims=True)
    small = []
    for dt, dw in PLANE:
        step = (dt, 0, dw)
        copy = links.copy(dots.at[1, 0], dots.at[1 - dt, side_of(dw)], number, step)
        number += 1
        pl.when(there(step))(copy.start)
        small.append((copy, there(step), there(back(step))))

    def clear(ref, *spot):
        ref[spot] = jnp.zeros(ref.shape[len(spot) :], ref.dtype)

    def clear_sums(x):
        for y in range(4):
            clear(dq, x, y)
        for y in range(2):
            clear(dk, x, y)
            clear(dv, x, y)

    for time in range(3):
        for spot in range(4):
            if (time, spot) not in ((1, 1), (1, 2)):

                @pl.when(jnp.logical_not(row_in[time] & col_in[spot]))
                def _():
                    clear(qa, time, spot)
                    clear(doa, time, spot)

    for row, step in ((0, H_DOWN), (2, H_UP)):

        @pl.when(jnp.logical_not(there(step)))
        def _():
            clear(ka, row)
            clear(va, row)

    def allowed(time, row):
        key_h = h + row - 1
        key_in = (key_h >= 0) & (key_h < nh)
        line = t * nh + jnp.clip(key_h, 0, nh - 1)
        found = []
        for col, shift in PAIRS:
            offset = 9 * (2 - time) + 3 * row + 2 - shift
            on = (active[line, 2 * w + col] == 1) & (pattern[0, offset] == 1)
            inside = key_in & row_in[time] & col_in[col + shift]
            found.append(inside & (on | (offset == 13)))
        return found

    def raise_scores(time, rows, spots):
        taken = [(row, col, shift) for row in rows for col, shift in PAIRS if col + shift in spots]
        scores = [dot(ka[row, col], qa[time, col + shift], NT) * factor for row, col, shift in taken]
        highs = [jnp.max(x, axis=0, keepdims=True) for x in scores]
        for (row, col, shift), x, high in zip(taken, scores, highs):
            x = jnp.exp2(x - high)
            raised[time, row, col, :, shift * tile : (shift + 1) * tile] = x.astype(BF16)
            line = 3 * col + shift
            tops[time, row, line : line + 1, :] = high
            sums[time, row, line : line + 1, :] = jnp.sum(x, axis=0, keepdims=True)

    def mask(time, row):
        lines = [jnp.full((1, tile), ok.astype(jnp.int32)) for ok in allowed(time, row)]
        return jnp.concatenate(lines, axis=0) == 1

    def by_spot(six, join):
        return jnp.concatenate([six[0:1], join(six[1:3], six[3:5]), six[5:6]], axis=0)

    def by_pair(four):
        return jnp.concatenate([four[0:3], four[1:4]], axis=0)

    def publish(time):
        nonlocal number
        highs = []
        for row in range(3):
            highs.append(jnp.where(mask(time, row), tops[time, row, 0:6, :], LOW))
        top = by_spot(functools.reduce(jnp.maximum, highs), jnp.maximum)
        total = 0.0
        for row in range(3):
            part = jnp.exp2(highs[row] - by_pair(top)) * sums[time, row, 0:6, :]
            total = total + jnp.where(mask(time, row), part, 0.0)
        total = by_spot(total, jnp.add)
        for half in range(2):
            inbox[time, time, 0, half, 0:2, :] = top[2 * half : 2 * half + 2]
            inbox[time, time, 0, half, 2:4, :] = total[2 * half : 2 * half + 2]
        for dt in (time - 2, time - 1, time):
            for dw in (-1, 0, 1):
                if (dt, dw) == (0, 0):
                    continue
                step = (dt, 0, dw)
                src, slot = inbox.at[time, time, 0], inbox.at[time - dt, time, 0]
                if dw:
                    half = (dw + 1) // 2
                    src, slot = src.at[half], inbox.at[time - dt, time, 1, 1 - half]
                copy = links.copy(src, slot, number, step)
                number += 1
                goes = row_in[time] & there(step)
                pl.when(goes)(copy.start)
                small.append((copy, goes, row_in[time - dt] & there(back(step))))

    def each(first, last, act):
        def step(x, carried):
            act(x)
            return carried

        lax.fori_loop(first, last, step, 0)

    own, outer = (1, 2), (0, 3)
    stay[2].wait()
    stay[3].wait()
    raise_scores(1, (1,), own)
    arrive(groups[0][2])
    send(groups[1][2])
    raise_scores(1, (0, 2), own)
    forward(groups[0])
    send(groups[1][1])
    raise_scores(1, (0, 1, 2), outer)
    publish(1)
    forward(groups[1])
    arrive(groups[0][1])
    each(0, 2, lambda x: raise_scores(2 * x, (0, 1, 2), own))
    for time in (0, 2):
        arrive([fan[:3] for fan in groups[0][3] if fan[3] == time])
        raise_scores(time, (0, 1, 2), outer)
        publish(time)
    each(0, 3, clear_sums)
    arrive(groups[1][1] + groups[1][2] + [fan[:3] for fan in groups[1][3]])
    stay[4].wait()
    arrive(small)

    for time in range(3):
        log_total = []
        for half, beside in ((0, w > 0), (1, w < nw - 1)):
            terms = []
            for sender in range(3):
                ok = (t + time - sender >= 0) & (t + time - sender < nt)
                for side, good in ((0, ok), (1, ok & beside)):
                    both = inbox[time, sender, side, half]
                    terms.append((jnp.where(good, both[0:2], LOW), jnp.where(good, both[2:4], 0.0)))
            top = functools.reduce(jnp.maximum, [x for x, _ in terms])
            log_total.append(top + jnp.log2(sum(y * jnp.exp2(x - top) for x, y in terms)))
        log_total = jnp.concatenate(log_total, axis=0)
        for row in range(3):
            part = jnp.exp2(tops[time, row, 0:6, :] - by_pair(log_total))
            sums[time, row, 0:6, :] = jnp.where(mask(time, row), part, 0.0)
        for spot, (side, line) in enumerate(((1, 1), (0, 0), (0, 1), (2, 0))):
            part = jnp.where(row_in[time] & col_in[spot], dots[time, side, line : line + 1, :], 0.0)
            for row in range(3):
                tops[time, row, spot : spot + 1, :] = part

    def gradients(time, row, parts=((0, 0, 3), (1, 0, 3))):
        for col, first, many in parts:
            begin, shifts = col + first, range(first, first + many)
            rows = qa[time, begin : begin + many].reshape(many * tile, -1)
            slopes = doa[time, begin : begin + many].reshape(many * tile, -1)
            weight = jnp.concatenate([sums[time, row, 3 * col + x : 3 * col + x + 1, :] for x in shifts], axis=1)
            middle = jnp.concatenate([tops[time, row, col + x : col + x + 1, :] for x in shifts], axis=1)
            probs = raised[time, row, col, :, first * tile : (first + many) * tile].astype(F32) * weight
            grads = (probs * (dot(va[row, col], slopes, NT) - middle)).astype(BF16)
            dv[row, col] += dot(probs.astype(BF16), slopes, NN)
            dk[row, col] += dot(grads, rows, NN)
            part = dot(ka[row, col], grads, TN)
            for x in range(many):
                dq[time, begin + x] += part[:, x * tile : (x + 1) * tile]

    returns = []
    for src, dst, step in (
        (send_k.at[0], key_in.at[1], H_DOWN),
        (send_v.at[0], value_in.at[1], H_DOWN),
        (send_k.at[1, 0], key_in.at[0, 0], H_UP),
        (send_v.at[1, 0], value_in.at[0, 0], H_UP),
        (send_k.at[1, 1], key_in.at[0, 1], H_UP),
        (send_v.at[1, 1], value_in.at[0, 1], H_UP),
        (send_q.at[0, pl.ds(1, 2)], time_in.at[1], T_DOWN),
        (send_q.at[0, 0], corner_in.at[1, 1], (-1, 0, -1)),
        (send_q.at[0, 3], corner_in.at[1, 0], (-1, 0, 1)),
        (send_q.at[1, pl.ds(1, 2)], time_in.at[0], T_UP),
        (send_q.at[1, 0], corner_in.at[0, 1], (1, 0, -1)),
        (send_q.at[1, 3], corner_in.at[0, 0], (1, 0, 1)),
        (edge.at[0], width_in.at[1], W_DOWN),
        (edge.at[1], width_in.at[0], W_UP),
    ):
        returns.append((links.copy(src, dst, number, step), there(step), there(back(step)), dst))
        number += 1

    def give(entries):
        for copy, goes, _, _ in entries:
            pl.when(goes)(copy.start)

    def take(entries):
        for copy, _, comes, dst in entries:

            @pl.when(jnp.logical_not(comes))
            def _():
                dst[...] = jnp.zeros(dst.shape, dst.dtype)

            pl.when(comes)(copy.wait_recv)

    each(0, 3, lambda x: gradients(2 * x % 3, 0))
    send_k[0] = dk[0].astype(BF16)
    send_v[0] = dv[0].astype(BF16)
    give(returns[0:2])

    def hand_over(turn):
        send_q[turn] = dq[2 * turn].astype(BF16)
        give(returns[6 + 3 * turn : 9 + 3 * turn])

    each(0, 2, lambda x: gradients(0, 2 - x))
    hand_over(0)
    gradients(2, 2)
    for col in range(2):
        gradients(1, 2, ((col, 0, 3),))
        send_k[1, col] = dk[2, col].astype(BF16)
        send_v[1, col] = dv[2, col].astype(BF16)
        give(returns[2 + 2 * col : 4 + 2 * col])
    gradients(2, 1)
    hand_over(1)
    gradients(1, 1, ((0, 0, 1), (1, 2, 1)))
    for turn, spot in ((0, 0), (1, 3)):
        edge[turn] = dq[1, spot].astype(BF16)
    give(returns[12:14])
    gradients(1, 1, ((0, 1, 2), (1, 0, 2)))
    take(returns[0:6])
    for spot in range(2):
        total = dk[1, spot] + key_in[0, spot].astype(F32) + key_in[1, spot].astype(F32)
        out_dk[spot] = (total * scale).astype(BF16)
        total = dv[1, spot] + value_in[0, spot].astype(F32) + value_in[1, spot].astype(F32)
        out_dv[spot] = total.astype(BF16)
    take(returns[6:14])
    for spot in range(2):
        total = dq[1, 1 + spot] + width_in[spot].astype(F32)
        for turn in range(2):
            total = total + time_in[turn, spot].astype(F32) + corner_in[turn, spot].astype(F32)
        out_dq[spot] = (total * scale).T.astype(BF16)
    for width, time, height, fans in groups:
        for copy, goes, _ in width + time + height + [fan[:3] for fan in fans]:
            pl.when(goes)(copy.wait_send)
    for copy, goes, _ in small + [x[:3] for x in returns]:
        pl.when(goes)(copy.wait_send)


def settle_kernel(*refs):
    ins, outs, held, sems = refs[:3], refs[3:6], refs[6:9], refs[9]
    first = [pltpu.make_async_copy(src, dst, sems.at[x]) for x, (src, dst) in enumerate(zip(ins, held))]
    then = [pltpu.make_async_copy(src, dst, sems.at[3 + x]) for x, (src, dst) in enumerate(zip(held, outs))]
    for copy in first:
        copy.start()
    for one, two in zip(first, then):
        one.wait()
        two.start()
    for copy in then:
        copy.wait()


def shape(*dims, dtype=BF16):
    return jax.ShapeDtypeStruct(dims, dtype)


def on_device(sizes, queries, key_tiles, value_tiles, forward_out, out_grad, pattern, tile_active):
    whole = queries.shape
    tile, feat = whole[4], whole[5]
    scale = 1.0 / math.sqrt(feat)
    q, k, v, fo, do = (
        x.reshape(2, tile, feat) for x in (queries, key_tiles, value_tiles, forward_out, out_grad)
    )
    active = tile_active.reshape(-1, tile_active.shape[2])
    hbm = pl.BlockSpec(memory_space=pltpu.HBM)
    vmem = pl.BlockSpec(memory_space=pltpu.VMEM)
    smem = pl.BlockSpec(memory_space=pltpu.SMEM)
    dma = pltpu.SemaphoreType.DMA

    dq, dk, dv = pl.pallas_call(
        functools.partial(attend_kernel, sizes, scale),
        out_shape=[shape(2, tile, feat)] * 3,
        in_specs=[smem] * 2 + [hbm] * 5,
        out_specs=[vmem] * 3,
        scratch_shapes=[
            pltpu.VMEM((3, 4, tile, feat), BF16),
            pltpu.VMEM((3, 4, tile, feat), BF16),
            pltpu.VMEM((3, 2, tile, feat), BF16),
            pltpu.VMEM((3, 2, tile, feat), BF16),
            pltpu.VMEM((2, tile, feat), BF16),
            pltpu.VMEM((3, 3, 2, 2, 4, tile), F32),
            pltpu.VMEM((3, 3, 2, tile), F32),
            pltpu.VMEM((3, 3, 8, tile), F32),
            pltpu.VMEM((3, 3, 8, tile), F32),
            pltpu.VMEM((3, 3, 2, tile, 3 * tile), BF16),
            pltpu.VMEM((3, 4, feat, tile), F32),
            pltpu.VMEM((3, 2, tile, feat), F32),
            pltpu.VMEM((3, 2, tile, feat), F32),
            pltpu.VMEM((2, 4, feat, tile), BF16),
            pltpu.VMEM((2, 2, tile, feat), BF16),
            pltpu.VMEM((2, 2, tile, feat), BF16),
            pltpu.VMEM((2, 2, feat, tile), BF16),
            pltpu.VMEM((2, 2, feat, tile), BF16),
            pltpu.VMEM((2, 2, tile, feat), BF16),
            pltpu.VMEM((2, 2, tile, feat), BF16),
            pltpu.VMEM((2, feat, tile), BF16),
            pltpu.VMEM((2, feat, tile), BF16),
            dma((5,)),
            dma((66,)),
            dma((66,)),
        ],
        compiler_params=pltpu.CompilerParams(
            collective_id=0, has_side_effects=True, vmem_limit_bytes=60 << 20
        ),
        name="attend",
    )(pattern, active, q, do, k, v, fo)
    dq, dk, dv = pl.pallas_call(
        settle_kernel,
        out_shape=[shape(2, tile, feat)] * 3,
        in_specs=[hbm] * 3,
        out_specs=[hbm] * 3,
        scratch_shapes=[pltpu.VMEM((2, tile, feat), BF16)] * 3 + [dma((6,))],
        compiler_params=pltpu.CompilerParams(vmem_limit_bytes=60 << 20),
        name="settle",
    )(dq, dk, dv)
    return dq.reshape(whole), dk.reshape(whole), dv.reshape(whole)


def solution(mesh):
    tiles = P("ta", "ha", "wa", None, None, None)
    sizes = tuple(mesh.shape[axis] for axis in ("ta", "ha", "wa"))
    return jax.shard_map(
        functools.partial(on_device, sizes),
        mesh=mesh,
        in_specs=(tiles,) * 5 + (P(), P()),
        out_specs=(tiles,) * 3,
        check_vma=False,
    )
```
